128 devices in a mesh: dp: 2 (over core), sect: 16 (over y, x), head: 4 (over z).
Axes of the slice: x: 4, y: 4, z: 4, core: 2. Of those that a mesh axis runs over, the one named last changes fastest.
Arguments:
- activations: bfloat16 [2, 4096, 4096], P('dp', 'sect'), may hold values from -6 to 6
- modality: int32 [2, 4096], P('dp', 'sect'), may hold values from 0 to 1, as said below
- query_rows: bfloat16 [2, 4096, 2048], P('dp', 'sect', 'head')
- key_rows: bfloat16 [2, 4096, 2048], P('dp', 'sect', 'head')
- value_weight: bfloat16 [2, 4096, 2048], P(None, 'sect', 'head'), may hold values from -0.09375 to 0.09375
- context_grad: bfloat16 [2, 4096, 2048], P('dp', 'sect', 'head'), may hold values from -6 to 6
Outputs:
- context: bfloat16 [2, 4096, 2048], P('dp', 'sect', 'head')
- input_grad: bfloat16 [2, 4096, 4096], P('dp', 'sect', 'head')
- weight_grad: float32 [2, 4096, 2048], P(None, 'sect', 'head')
The draws below stay inside these ranges and needn't reach their ends.
Inputs may be any that keep to these rules, and one draw needn't show every extreme that they name: `modality`: each sequence holds exactly one image span of 1024 positions (value 1) that starts at a multiple of 128; every other position is text (value 0).
All inputs are finite; a program needn't handle non-finite values.
Results may differ from the reference program's by a relative error of at most 0.015.
Values may be sent and summed in bfloat16 or wider, within the bound.
A program may use at most 128 MiB of HBM per device.

```python
import jax
import jax.numpy as jnp
from jax import lax

D = 4096
HEADS = 16
HD = 128
BLOCK = 128
IMG = 1024
LENGTH = 4096
NSEQ = 2


def shared_normals(key):
    return jax.random.normal(key, (NSEQ, LENGTH, HEADS * HD), jnp.float32)


def draw_modality(key, part):
    key = jax.random.fold_in(key, 5)
    start_slots = (LENGTH - IMG) // BLOCK + 1
    span_start = BLOCK * jax.random.randint(key, (NSEQ, 1), 0, start_slots)
    positions = jnp.arange(LENGTH)[None, :]
    return ((positions >= span_start) & (positions < span_start + IMG)).astype(jnp.int32)


def draw_key_rows(key, part):
    shared = shared_normals(key)
    return shared.astype(jnp.bfloat16)


def draw_query_rows(key, part):
    key = jax.random.fold_in(key, 23)
    fresh = jax.random.normal(key, (NSEQ, LENGTH, HEADS * HD), jnp.float32)
    return fresh.astype(jnp.bfloat16)


def levels(stream_key, dims, shards, low, largest):
    level, own = 1.0, jax.random.fold_in(stream_key, 6)
    for position, shards_of in shards:
        steps = jnp.exp(jax.random.uniform(jax.random.fold_in(own, position), (shards_of,), jnp.float32, low / len(shards), largest / len(shards)))
        level = level * jnp.repeat(steps, dims[position] // shards_of).reshape([-1 if axis == position else 1 for axis in range(len(dims))])
    return level


def gaussian(key, shape, scale, bound, shards=(), dtype=jnp.bfloat16):
    result = scale * jax.random.normal(key, shape, jnp.float32)
    if shards:
        result = result * levels(key, shape, shards, -0.22, 0.18)
    return jnp.clip(result, -bound, bound).astype(dtype)


def setup_inputs(seed: int = 0) -> dict:
    key_of = jax.random.split(jax.random.key(seed), 7)
    return {
        "activations": gaussian(key_of[0], (NSEQ, LENGTH, D), 1.0, 6.0, ((0, 2), (1, 16))),
        "modality": draw_modality(jax.random.fold_in(key_of[6], 71), 0),
        "query_rows": draw_query_rows(jax.random.fold_in(key_of[6], 71), 0),
        "key_rows": draw_key_rows(jax.random.fold_in(key_of[6], 71), 0),
        "value_weight": gaussian(key_of[4], (2, D, HEADS * HD), D ** -0.5, 0.09375, ((1, 16), (2, 4))),
        "context_grad": gaussian(key_of[5], (NSEQ, LENGTH, HEADS * HD), 1.0, 6.0, ((0, 2), (1, 16), (2, 4))),
    }


def pick_product(blocks, block_kinds, weights):
    def single(entry):
        block_rows, block_kind = entry
        chosen = lax.dynamic_index_in_dim(weights, block_kind, 0, keepdims=False)
        return jnp.dot(block_rows, chosen, preferred_element_type=jnp.float32)
    return lax.map(single, (blocks, block_kinds))


def reference(activations, modality, query_rows, key_rows, value_weight, context_grad):
    seq_count, full_length, feat_width = activations.shape
    inner_width = value_weight.shape[2]
    head_count = inner_width // HD
    score_scale = HD ** -0.5
    block_kinds = modality[:, ::BLOCK].reshape(-1).astype(jnp.int32)
    feature_blocks = activations.reshape(-1, BLOCK, feat_width)
    value = pick_product(feature_blocks, block_kinds, value_weight).astype(jnp.bfloat16)
    value = value.reshape(seq_count, full_length, inner_width)
    positions = jnp.arange(full_length)
    allowed = positions[:, None] >= positions[None, :]

    def split_heads(array):
        shaped = array.reshape(seq_count, full_length, head_count, HD).transpose(0, 2, 1, 3)
        return shaped.reshape(seq_count * head_count, full_length, HD)

    def join_heads(array):
        shaped = array.reshape(seq_count, head_count, full_length, HD).transpose(0, 2, 1, 3)
        return shaped.reshape(seq_count, full_length, inner_width)

    def attend(entry):
        queries, keys_here, values_here, grads_here = entry
        scores = jnp.dot(queries, keys_here.T, preferred_element_type=jnp.float32) * score_scale
        scores = jnp.where(allowed, scores, -1e30)
        highest = jnp.max(scores, axis=1, keepdims=True)
        powers = jnp.exp(scores - highest)
        probs = (powers / jnp.sum(powers, axis=1, keepdims=True)).astype(jnp.bfloat16)
        context_here = jnp.dot(probs, values_here, preferred_element_type=jnp.float32).astype(jnp.bfloat16)
        value_grad_here = jnp.dot(probs.T, grads_here, preferred_element_type=jnp.float32).astype(jnp.bfloat16)
        return context_here, value_grad_here

    context_heads, value_grad_heads = lax.map(attend, (split_heads(query_rows), split_heads(key_rows), split_heads(value), split_heads(context_grad)))
    context = join_heads(context_heads)
    value_grad = join_heads(value_grad_heads)
    grad_blocks = value_grad.reshape(-1, BLOCK, inner_width)

    def accumulate(running, entry):
        block_rows, block_grads, block_kind = entry
        current = lax.dynamic_index_in_dim(running, block_kind, 0, keepdims=False)
        update = current + jnp.dot(block_rows.T, block_grads, preferred_element_type=jnp.float32)
        back_rows = jnp.dot(block_grads, lax.dynamic_index_in_dim(value_weight, block_kind, 0, keepdims=False).T, preferred_element_type=jnp.float32)
        return lax.dynamic_update_index_in_dim(running, update, block_kind, 0), back_rows

    start_grad = jnp.zeros((2, feat_width, inner_width), jnp.float32)
    weight_grad, back_blocks = lax.scan(accumulate, start_grad, (feature_blocks, grad_blocks, block_kinds))
    input_grad = back_blocks.reshape(seq_count, full_length, feat_width).astype(jnp.bfloat16)
    return (context, input_grad, weight_grad)
```

```python
import functools

import jax
import jax.numpy as jnp
from jax import lax
from jax.experimental import pallas as pl
from jax.experimental.pallas import tpu as pltpu
from jax.sharding import PartitionSpec as P

HD = 128
BLOCK = 128
SCALE = HD ** (-0.5)
EXP2_SCALE = SCALE * 1.4426950408889634
NEG = -1e30
MESH = pl.DeviceIdType.MESH
F32 = jnp.float32
BF16 = jnp.bfloat16

T = 256
C = 512
F = 1024
NH = C // HD


def dot(a, b, ca, cb):
    return lax.dot_general(a, b, (((ca,), (cb,)), ((), ())), preferred_element_type=F32)


def kernel(
    act, mod, qin, kin, win, gin,
    ctx_out, ig_out, wg_out,
    mod_v, mg, ag, wg, qg, gg, kg, vg,
    pt, st, gs,
    dvp, dvf, dvr, dv,
    vp, vf, vr,
    cp, cf, cr, co,
    ip, if_, ir, igs, igo,
    wother, wrecv, wown, wsend, wr, wo,
    loc_sem,
    s_mod, r_mod, s_act, r_act, s_actz, r_actz, s_k, r_k, s_q, r_q, s_g, r_g, s_w, r_w, s_wc, r_wc,
    s_st, r_st, s_dv, r_dv, s_dvg, r_dvg, s_v, r_v, s_vg, r_vg, s_c, r_c, s_i, r_i, s_t, r_t,
    s_wx, r_wx, s_wr, r_wr, s_wo, r_wo,
):
    c = lax.axis_index("dp")
    s = lax.axis_index("sect")
    z = lax.axis_index("head")
    y = s // 4
    x = lax.rem(s, 4)

    def wrap(v):
        return lax.rem(v + 4, 4)

    def on_x(d):
        return (c, y * 4 + wrap(x + d), z)

    def on_y(d):
        return (c, wrap(y + d) * 4 + x, z)

    def on_z(d):
        return (c, s, wrap(z + d))

    partner = (1 - c, s, z)
    across = (c, z * 4 + x, y)

    sends = []

    def remote(src, dst, ssem, rsem, dev):
        copy = pltpu.make_async_remote_copy(
            src_ref=src, dst_ref=dst, send_sem=ssem, recv_sem=rsem, device_id=dev, device_id_type=MESH
        )
        copy.start()
        sends.append(copy)
        return copy

    local = [
        pltpu.make_async_copy(mod, mod_v, loc_sem.at[0]),
        pltpu.make_async_copy(act.at[0, :, pl.ds(pl.multiple_of(y * F, F), F)], ag.at[y], loc_sem.at[1]),
        pltpu.make_async_copy(qin.at[0], qg.at[x], loc_sem.at[2]),
        pltpu.make_async_copy(kin.at[0], kg.at[y], loc_sem.at[3]),
        pltpu.make_async_copy(gin.at[0], gg.at[x], loc_sem.at[4]),
        pltpu.make_async_copy(win.at[0], wg.at[0, x], loc_sem.at[5]),
        pltpu.make_async_copy(win.at[1], wg.at[1, x], loc_sem.at[6]),
    ]
    for copy in local:
        copy.start()

    barrier = pltpu.get_barrier_semaphore()
    for d in (1, 2, 3):
        for dev in (on_x(d), on_y(d), on_z(d)):
            pl.semaphore_signal(barrier, inc=1, device_id=dev, device_id_type=MESH)
    pl.semaphore_signal(barrier, inc=1, device_id=partner, device_id_type=MESH)

    @pl.when(y != z)
    def _():
        pl.semaphore_signal(barrier, inc=1, device_id=across, device_id_type=MESH)

    pl.semaphore_wait(barrier, jnp.where(y != z, 11, 10))

    a_y, q_x, k_y, g_x, w_x = [], [], [], [], []
    quarter = pl.ds(pl.multiple_of(z * (T // 4), T // 4), T // 4)
    for d in (1, 3, 2):
        group = pl.ds(pl.multiple_of(wrap(y + d) * F, F), F)
        a_y.append(
            remote(act.at[0, quarter, group], ag.at[y, quarter], s_act.at[d - 1], r_act.at[d - 1], on_y(d))
        )
    for d in (1, 3, 2):
        q_x.append(remote(qin.at[0], qg.at[x], s_q.at[d - 1], r_q.at[d - 1], on_x(d)))
    for d in (1, 3, 2):
        k_y.append(remote(kin.at[0], kg.at[y], s_k.at[d - 1], r_k.at[d - 1], on_y(d)))

    local[0].wait()
    mg[y] = jnp.broadcast_to(mod_v[...], (8, T))
    m_y = [remote(mg.at[y], mg.at[y], s_mod.at[d - 1], r_mod.at[d - 1], on_y(d)) for d in (1, 2, 3)]

    a_z = []
    for n, d in enumerate((1, 3, 2)):
        a_y[n].wait_recv()
        piece = ag.at[wrap(y - d), quarter]
        for e in (1, 3, 2):
            a_z.append(remote(piece, piece, s_actz.at[d - 1, e - 1], r_actz.at[d - 1, e - 1], on_z(e)))

    for d in (1, 3, 2):
        g_x.append(remote(gin.at[0], gg.at[x], s_g.at[d - 1], r_g.at[d - 1], on_x(d)))
    for d in (1, 3, 2):
        w_x.append(remote(win.at[c], wg.at[c, x], s_w.at[d - 1], r_w.at[d - 1], on_x(d)))

    for copy in local[1:]:
        copy.wait()
    for copy in q_x + k_y:
        copy.wait_recv()

    key_pos = lax.broadcasted_iota(jnp.int32, (T, T), 0)
    query_pos = lax.broadcasted_iota(jnp.int32, (T, T), 1)
    ahead = query_pos - key_pos

    def score_block(p, _):
        cols = pl.ds(pl.multiple_of(p * T, T), T)
        for h in range(NH):
            hs = slice(h * HD, (h + 1) * HD)
            parts = []
            for q in range(4):
                sc = dot(kg[q, :, hs], qg[p, :, hs], 1, 1)
                parts.append(jnp.where(ahead >= (4 * q + x - 4 * y - p) * T, sc, NEG))
            top = functools.reduce(jnp.maximum, [jnp.max(v, axis=0, keepdims=True) for v in parts])
            total = jnp.zeros((1, T), F32)
            for q in range(4):
                pw = jnp.exp2((parts[q] - top) * EXP2_SCALE)
                total = total + jnp.sum(pw, axis=0, keepdims=True)
                pt[h, q * T:(q + 1) * T, cols] = pw.astype(BF16)
            st[x, h:h + 1, cols] = top
            st[x, NH + h:NH + h + 1, cols] = total
        return 0

    lax.fori_loop(0, 4, score_block, 0)
    st_x = [remote(st.at[x], st.at[x], s_st.at[d - 1], r_st.at[d - 1], on_x(d)) for d in (1, 3, 2)]
    for copy in st_x:
        copy.wait_recv()
    tops = [st[n, 0:NH, :] for n in range(4)]
    top = functools.reduce(jnp.maximum, tops)
    total = jnp.zeros_like(top)
    for n in range(4):
        total = total + st[n, NH:2 * NH, :] * jnp.exp2((tops[n] - top) * EXP2_SCALE)
    factor = jnp.exp2((st[x, 0:NH, :] - top) * EXP2_SCALE) / total

    for copy in g_x:
        copy.wait_recv()
    for h in range(NH):
        hs = slice(h * HD, (h + 1) * HD)
        for p in range(4):
            wide = jnp.broadcast_to(factor[h:h + 1, p * T:(p + 1) * T], (HD, T)).T
            gs[p * T:(p + 1) * T, hs] = (gg[p, :, hs].astype(F32) * wide).astype(BF16)

    dv_y = []
    for e in (1, 3, 2, 0):
        q = wrap(y + e)
        rows = pl.ds(pl.multiple_of(q * T, T), T)
        for h in range(NH):
            hs = slice(h * HD, (h + 1) * HD)
            part = dot(pt[h, rows, :], gs[:, hs], 1, 0)
            if e:
                dvp[e - 1, :, hs] = part.astype(BF16)
            else:
                dvf[:, hs] = part
        if e:
            dv_y.append(remote(dvp.at[e - 1], dvr.at[e - 1], s_dv.at[e - 1], r_dv.at[e - 1], on_y(e)))

    w_c = []
    for n, d in enumerate((1, 3, 2)):
        w_x[n].wait_recv()
        block = wg.at[c, wrap(x - d)]
        w_c.append(remote(block, block, s_wc.at[d - 1], r_wc.at[d - 1], partner))
    for copy in m_y + a_z:
        copy.wait_recv()
    for copy in w_c:
        copy.wait_recv()

    def image_rows(q, width):
        parts = []
        for b in range(T // BLOCK):
            row = mg[q, 0:1, b * BLOCK:(b + 1) * BLOCK]
            row = jnp.concatenate([row] * (width // BLOCK), axis=1)
            parts.append(jnp.broadcast_to(row, (BLOCK, width)))
        return jnp.concatenate(parts, axis=0) == 1

    def value_part(q):
        rows = ag[q]
        text = dot(rows, wg[0].reshape(F, C), 1, 0)
        image = dot(rows, wg[1].reshape(F, C), 1, 0)
        return jnp.where(image_rows(q, C), image, text)

    v_y = []
    for e in (1, 3, 2, 0):
        part = value_part(wrap(y + e))
        if e:
            vp[e - 1] = part.astype(BF16)
            v_y.append(remote(vp.at[e - 1], vr.at[e - 1], s_v.at[e - 1], r_v.at[e - 1], on_y(e)))
        else:
            vf[...] = part

    for copy in dv_y:
        copy.wait_recv()
    dv[y] = (dvf[...] + dvr[0].astype(F32) + dvr[1].astype(F32) + dvr[2].astype(F32)).astype(BF16)
    dvg_y = [remote(dv.at[y], dv.at[y], s_dvg.at[d - 1], r_dvg.at[d - 1], on_y(d)) for d in (1, 3, 2)]
    for copy in v_y:
        copy.wait_recv()
    vg[y] = (vf[...] + vr[0].astype(F32) + vr[1].astype(F32) + vr[2].astype(F32)).astype(BF16)
    vg_y = [remote(vg.at[y], vg.at[y], s_vg.at[d - 1], r_vg.at[d - 1], on_y(d)) for d in (1, 3, 2)]

    for copy in dvg_y:
        copy.wait_recv()

    def back_part(q):
        rows = dv[q]
        text = dot(rows, wg[0].reshape(F, C), 1, 1)
        image = dot(rows, wg[1].reshape(F, C), 1, 1)
        return jnp.where(image_rows(q, F), image, text)

    i_z = []
    for e in (1, 3, 2, 0):
        part = back_part(wrap(z + e))
        if e:
            ip[e - 1] = part.astype(BF16)
            i_z.append(remote(ip.at[e - 1], ir.at[e - 1], s_i.at[e - 1], r_i.at[e - 1], on_z(e)))
        else:
            if_[...] = part

    feats = ag[...].reshape(4 * T, F)

    def update(kind):
        masked = [
            jnp.where(image_rows(q, C) == (kind == 1), dv[q].astype(F32), 0.0).astype(BF16) for q in range(4)
        ]
        return dot(feats, jnp.concatenate(masked, axis=0), 0, 0)

    wother[...] = update(1 - c).astype(BF16)
    wx = remote(wother, wrecv, s_wx.at[0], r_wx.at[0], partner)
    wown[...] = update(c)
    wx.wait_recv()
    wr_x = []
    for e in (1, 3, 2, 0):
        rows = pl.ds(pl.multiple_of(wrap(x + e) * T, T), T)
        summed = wown[rows, :] + wrecv[rows, :].astype(F32)
        if e:
            wsend[e - 1] = summed.astype(BF16)
            wr_x.append(remote(wsend.at[e - 1], wr.at[e - 1], s_wr.at[e - 1], r_wr.at[e - 1], on_x(e)))
        else:
            own_update = summed
            wo[c] = own_update

    for copy in vg_y:
        copy.wait_recv()
    values = vg[...].reshape(4 * T, C)
    c_x = []
    for e in (1, 3, 2, 0):
        p = wrap(x + e)
        cols = pl.ds(pl.multiple_of(p * T, T), T)
        for h in range(NH):
            hs = slice(h * HD, (h + 1) * HD)
            part = dot(values[:, hs], pt[h, :, cols], 0, 0)
            top_p = functools.reduce(jnp.maximum, [st[n, h:h + 1, cols] for n in range(4)])
            total_p = jnp.zeros_like(top_p)
            for n in range(4):
                total_p = total_p + st[n, NH + h:NH + h + 1, cols] * jnp.exp2(
                    (st[n, h:h + 1, cols] - top_p) * EXP2_SCALE
                )
            factor_p = jnp.exp2((st[x, h:h + 1, cols] - top_p) * EXP2_SCALE) / total_p
            part = (part * factor_p).T
            if e:
                cp[e - 1, :, hs] = part.astype(BF16)
            else:
                cf[:, hs] = part
        if e:
            c_x.append(remote(cp.at[e - 1], cr.at[e - 1], s_c.at[e - 1], r_c.at[e - 1], on_x(e)))

    for copy in i_z:
        copy.wait_recv()
    summed = (if_[...] + ir[0].astype(F32) + ir[1].astype(F32) + ir[2].astype(F32)).astype(BF16)

    @pl.when(y == z)
    def _():
        igo[...] = summed

    @pl.when(y != z)
    def _():
        igs[...] = summed
        pltpu.make_async_remote_copy(
            src_ref=igs, dst_ref=igo, send_sem=s_t.at[0], recv_sem=r_t.at[0], device_id=across, device_id_type=MESH
        ).start()

    for copy in wr_x:
        copy.wait_recv()
    wo[c] = wo[c] + wr[0].astype(F32) + wr[1].astype(F32) + wr[2].astype(F32)
    w_out = remote(wo.at[c], wo.at[c], s_wo.at[0], r_wo.at[0], partner)

    for copy in c_x:
        copy.wait_recv()
    co[...] = (cf[...] + cr[0].astype(F32) + cr[1].astype(F32) + cr[2].astype(F32)).astype(BF16)
    out_c = pltpu.make_async_copy(co, ctx_out, loc_sem.at[0])
    out_c.start()

    @pl.when(y != z)
    def _():
        copy = pltpu.make_async_remote_copy(
            src_ref=igs, dst_ref=igo, send_sem=s_t.at[0], recv_sem=r_t.at[0], device_id=across, device_id_type=MESH
        )
        copy.wait()

    out_i = pltpu.make_async_copy(igo, ig_out, loc_sem.at[1])
    out_i.start()
    w_out.wait_recv()
    out_w = pltpu.make_async_copy(wo, wg_out, loc_sem.at[2])
    out_w.start()
    for copy in sends:
        copy.wait_send()
    out_c.wait()
    out_i.wait()
    out_w.wait()


def shards(activations, modality, query_rows, key_rows, value_weight, context_grad):
    vm = lambda shape, dtype=BF16: pltpu.VMEM(shape, dtype)
    dma = lambda *shape: pltpu.SemaphoreType.DMA(shape)
    any_spec = pl.BlockSpec(memory_space=pl.ANY)
    three = [dma(3), dma(3)]
    ctx, ig, wgrad = pl.pallas_call(
        kernel,
        out_shape=(
            jax.ShapeDtypeStruct((T, C), BF16),
            jax.ShapeDtypeStruct((T, F), BF16),
            jax.ShapeDtypeStruct((2, T, C), F32),
        ),
        in_specs=[any_spec] * 6,
        out_specs=(any_spec,) * 3,
        scratch_shapes=[
            vm((1, T), jnp.int32), vm((4, 8, T), jnp.int32), vm((4, T, F)), vm((2, 4, T, C)),
            vm((4, T, C)), vm((4, T, C)), vm((4, T, C)), vm((4, T, C)),
            vm((NH, 4 * T, 4 * T)), vm((4, 8, 4 * T), F32), vm((4 * T, C)),
            vm((3, T, C)), vm((T, C), F32), vm((3, T, C)), vm((4, T, C)),
            vm((3, T, C)), vm((T, C), F32), vm((3, T, C)),
            vm((3, T, C)), vm((T, C), F32), vm((3, T, C)), vm((T, C)),
            vm((3, T, F)), vm((T, F), F32), vm((3, T, F)), vm((T, F)), vm((T, F)),
            vm((F, C)), vm((F, C)), vm((F, C), F32), vm((3, T, C)), vm((3, T, C)), vm((2, T, C), F32),
            dma(7),
            *three, *three, dma(3, 3), dma(3, 3), *three, *three, *three, *three, *three,
            *three, *three, *three, *three, *three, *three, *three, dma(1), dma(1),
            dma(1), dma(1), *three, dma(1), dma(1),
        ],
        compiler_params=pltpu.CompilerParams(
            collective_id=0, has_side_effects=True, vmem_limit_bytes=60 * 2**20
        ),
        name="routed_attention",
    )(activations, modality, query_rows, key_rows, value_weight, context_grad)
    return ctx[None], ig[None], wgrad


def solution(mesh):
    return jax.shard_map(
        shards,
        mesh=mesh,
        in_specs=(
            P("dp", "sect", None),
            P("dp", "sect"),
            P("dp", "sect", "head"),
            P("dp", "sect", "head"),
            P(None, "sect", "head"),
            P("dp", "sect", "head"),
        ),
        out_specs=(P("dp", "sect", "head"), P("dp", "sect", "head"), P(None, "sect", "head")),
        check_vma=False,
    )
```

```python
import functools

import jax
import jax.numpy as jnp
from jax import lax
from jax.experimental import pallas as pl
from jax.experimental.pallas import tpu as pltpu
from jax.sharding import PartitionSpec as P

HD = 128
BLOCK = 128
EXP2_SCALE = HD ** (-0.5) * 1.4426950408889634
NEG = -1e30
MESH = pl.DeviceIdType.MESH
F32 = jnp.float32
BF16 = jnp.bfloat16

T = 256
C = 512
F = 1024
FB = 256
NH = C // HD


def dot(a, b, ca, cb):
    return lax.dot_general(a, b, (((ca,), (cb,)), ((), ())), preferred_element_type=F32)


def wrap(v):
    return lax.rem(v + 4, 4)


def kernel(
    act, mod, qin, kin, win, gin,
    ctx_out, ig_out, wg_out,
    mod_v, mg, ag, wg, qg, gg, kg, vg, dv,
    pt, st, fa, gs,
    d_part, d_in, d_own,
    v_part, v_in, v_own,
    c_part, c_in, c_own, co,
    i_part, i_in, i_own, igs, igo,
    w_other, w_recv, w_own, w_mine, w_part, w_in, wo,
    loc_sem, sems, ssem_t, rsem_t,
):
    c = lax.axis_index("dp")
    s = lax.axis_index("sect")
    z = lax.axis_index("head")
    y = s // 4
    x = lax.rem(s, 4)

    def on_x(d):
        return (c, y * 4 + wrap(x + d), z)

    def on_y(d):
        return (c, wrap(y + d) * 4 + x, z)

    def on_z(d):
        return (c, s, wrap(z + d))

    partner = (1 - c, s, z)
    sends = []
    used = [0]

    def remote(src, dst, dev):
        n = used[0]
        used[0] += 1
        copy = pltpu.make_async_remote_copy(
            src_ref=src, dst_ref=dst, send_sem=sems.at[0, n], recv_sem=sems.at[1, n],
            device_id=dev, device_id_type=MESH,
        )
        copy.start()
        sends.append(copy)
        return copy

    class Gather:
        def __init__(self, on, slot, fixed=False):
            self.on, self.slot, self.fixed = on, slot, fixed

        def there(self, d, part, step):
            return self.slot(d, part) if self.fixed else self.slot((d + step) % 4, part)

        def start(self, own=None):
            on, there = self.on, self.there
            own = own or (lambda part: self.slot(0, part))
            self.a_up = remote(own(0), there(0, 0, 1), on(1))
            self.b_dn = remote(own(1), there(0, 1, -1), on(-1))
            self.b_up = remote(own(1), there(0, 1, 1), on(1))
            self.a_dn = remote(own(0), there(0, 0, -1), on(-1))

        def relay(self):
            on, there = self.on, self.there
            self.a_up.wait_recv()
            self.a_far = remote(self.slot(1, 0), there(1, 0, 1), on(1))
            self.b_dn.wait_recv()
            self.b_far = remote(self.slot(3, 1), there(3, 1, -1), on(-1))

        def finish(self):
            for copy in (self.b_up, self.a_dn, self.a_far, self.b_far):
                copy.wait_recv()

    def gather(on, buf, rows):
        half = rows // 2
        return Gather(on, lambda d, part: buf.at[d, pl.ds(part * half, half)])

    class Sum:
        def __init__(self, on, part, inbox, half):
            self.on, self.part, self.inbox, self.half = on, part, inbox, half
            self.a, self.b = pl.ds(0, half), pl.ds(half, half)

        def far(self):
            self.f_up = remote(self.part.at[1, self.a], self.inbox.at[0], self.on(1))
            self.f_dn = remote(self.part.at[1, self.b], self.inbox.at[1], self.on(-1))

        def near_up(self):
            self.n_up = remote(self.part.at[0, self.b], self.inbox.at[2], self.on(1))

        def near_dn(self):
            self.n_dn = remote(self.part.at[2, self.a], self.inbox.at[3], self.on(-1))

        def relay(self):
            self.f_up.wait_recv()
            self.part[0, self.a] = (self.part[0, self.a].astype(F32) + self.inbox[0].astype(F32)).astype(BF16)
            self.s_up = remote(self.part.at[0, self.a], self.inbox.at[4], self.on(1))
            self.f_dn.wait_recv()
            self.part[2, self.b] = (self.part[2, self.b].astype(F32) + self.inbox[1].astype(F32)).astype(BF16)
            self.s_dn = remote(self.part.at[2, self.b], self.inbox.at[5], self.on(-1))

        def finish(self, own):
            for copy in (self.n_up, self.n_dn, self.s_up, self.s_dn):
                copy.wait_recv()
            first = own[self.a] + self.inbox[4].astype(F32) + self.inbox[3].astype(F32)
            second = own[self.b] + self.inbox[2].astype(F32) + self.inbox[5].astype(F32)
            return first, second

    local = [
        pltpu.make_async_copy(mod, mod_v, loc_sem.at[0]),
        pltpu.make_async_copy(act.at[0, :, pl.ds(pl.multiple_of(y * F, F), F)], ag.at[0], loc_sem.at[1]),
        pltpu.make_async_copy(qin.at[0], qg.at[0], loc_sem.at[2]),
        pltpu.make_async_copy(kin.at[0], kg.at[0], loc_sem.at[3]),
        pltpu.make_async_copy(gin.at[0], gg.at[0], loc_sem.at[4]),
        pltpu.make_async_copy(win.at[0], wg.at[0, x], loc_sem.at[5]),
        pltpu.make_async_copy(win.at[1], wg.at[1, x], loc_sem.at[6]),
    ]
    for copy in local:
        copy.start()

    barrier = pltpu.get_barrier_semaphore()
    for d in (1, 2, 3):
        for dev in (on_x(d), on_y(d), on_z(d)):
            pl.semaphore_signal(barrier, inc=1, device_id=dev, device_id_type=MESH)
    pl.semaphore_signal(barrier, inc=1, device_id=partner, device_id_type=MESH)
    for n in range(4):

        @pl.when(jnp.logical_and(n != y, y != z))
        def _(n=n):
            pl.semaphore_signal(barrier, inc=1, device_id=(c, n * 4 + x, y), device_id_type=MESH)

        @pl.when(jnp.logical_and(n != z, y != z))
        def _(n=n):
            pl.semaphore_signal(barrier, inc=1, device_id=(c, z * 4 + x, n), device_id_type=MESH)

    pl.semaphore_wait(barrier, jnp.where(y != z, 16, 10))

    def hbm_half(ref):
        return lambda part: ref.at[0, pl.ds(part * (T // 2), T // 2)]

    q_all, k_all = gather(on_x, qg, T), gather(on_y, kg, T)
    g_all = gather(on_x, gg, T)
    k_all.start(hbm_half(kin))
    q_all.start(hbm_half(qin))

    local[0].wait()
    mg[0] = jnp.broadcast_to(mod_v[...], (8, T))
    m_y = [remote(mg.at[0], mg.at[d], on_y(d)) for d in (1, 2, 3)]
    k_all.relay()
    q_all.relay()
    for copy in local[1:]:
        copy.wait()
    k_all.finish()
    q_all.finish()

    g_all.start(hbm_half(gin))
    quarter = pl.ds(pl.multiple_of(z * (T // 4), T // 4), T // 4)
    a_y = []
    for d in (1, 3, 2):
        group = pl.ds(pl.multiple_of(wrap(y + d) * F, F), F)
        a_y.append(remote(act.at[0, quarter, group], ag.at[d, quarter], on_y(d)))

    key_pos = lax.broadcasted_iota(jnp.int32, (T, T), 0)
    query_pos = lax.broadcasted_iota(jnp.int32, (T, T), 1)
    ahead = query_pos - key_pos

    def score_block(a, _):
        p = wrap(x - a)
        cols = pl.ds(pl.multiple_of(a * T, T), T)
        for h in range(NH):
            hs = slice(h * HD, (h + 1) * HD)
            parts = []
            for b in range(4):
                sc = dot(kg[b, :, hs], qg[a, :, hs], 1, 1)
                parts.append(jnp.where(ahead >= (4 * wrap(y - b) + x - 4 * y - p) * T, sc, NEG))
            top = functools.reduce(jnp.maximum, [jnp.max(v, axis=0, keepdims=True) for v in parts])
            total = jnp.zeros((1, T), F32)
            for b in range(4):
                pw = jnp.exp2((parts[b] - top) * EXP2_SCALE)
                total = total + jnp.sum(pw, axis=0, keepdims=True)
                pt[h, b * T:(b + 1) * T, cols] = pw.astype(BF16)
            st[0, p, h:h + 1, :] = top
            st[0, p, NH + h:NH + h + 1, :] = total
        return 0

    lax.fori_loop(0, 2, score_block, 0)
    g_all.relay()
    lax.fori_loop(2, 4, score_block, 0)
    st_x = [remote(st.at[0], st.at[d], on_x(d)) for d in (1, 3, 2)]

    w_all = Gather(on_x, lambda d, part: wg.at[c, wrap(x - d), pl.ds(part * (FB // 2), FB // 2)], fixed=True)
    w_all.start(lambda part: win.at[c, pl.ds(part * (FB // 2), FB // 2)])
    for copy in a_y:
        copy.wait_recv()

    def z_slot(d, part):
        rows = pl.ds(pl.multiple_of(wrap(z - d) * (T // 4) + part * (T // 8), T // 8), T // 8)
        return ag.at[pl.ds(1, 3), rows]

    a_all = Gather(on_z, z_slot, fixed=True)
    a_all.start()

    for copy in st_x:
        copy.wait_recv()
    for a in range(4):
        p = wrap(x - a)
        tops = [st[d, p, 0:NH] for d in range(4)]
        top = functools.reduce(jnp.maximum, tops)
        total = jnp.zeros_like(top)
        for d in range(4):
            total = total + st[d, p, NH:2 * NH] * jnp.exp2((tops[d] - top) * EXP2_SCALE)
        each = jnp.exp2((tops[0] - top) * EXP2_SCALE) / total
        for h in range(NH):
            fa[a, h] = jnp.broadcast_to(each[h:h + 1], (8, T))

    def factor(a, h):
        return jnp.concatenate([fa[a, h]] * (HD // 8), axis=0)

    g_all.finish()
    for h in range(NH):
        hs = slice(h * HD, (h + 1) * HD)
        for a in range(4):
            wide = factor(a, h).T
            gs[a * T:(a + 1) * T, hs] = (gg[a, :, hs].astype(F32) * wide).astype(BF16)

    d_sum = Sum(on_y, d_part, d_in, T // 2)

    def d_block(e):
        b = (4 - e) % 4
        for h in range(NH):
            hs = slice(h * HD, (h + 1) * HD)
            part = dot(pt[h, b * T:(b + 1) * T, :], gs[:, hs], 1, 0)
            if e:
                d_part[e - 1, :, hs] = part.astype(BF16)
            else:
                d_own[:, hs] = part

    d_block(2)
    d_sum.far()
    d_block(1)
    d_sum.near_up()
    d_block(3)
    d_sum.near_dn()
    a_all.relay()
    d_block(0)
    w_all.relay()
    d_sum.relay()
    w_all.finish()
    w_c = [remote(wg.at[c, wrap(x - d)], wg.at[c, wrap(x - d)], partner) for d in (1, 2, 3)]
    first, second = d_sum.finish(d_own)
    dv[0, 0:T // 2] = first.astype(BF16)
    dv[0, T // 2:T] = second.astype(BF16)
    d_all = gather(on_y, dv, T)
    d_all.start()

    def image_rows(b, width):
        parts = []
        for n in range(T // BLOCK):
            tile = mg[b, :, n * BLOCK:(n + 1) * BLOCK]
            tile = jnp.concatenate([tile] * (width // BLOCK), axis=1)
            parts += [tile] * (BLOCK // 8)
        return jnp.concatenate(parts, axis=0) == 1

    a_all.finish()
    for copy in (*m_y, *w_c):
        copy.wait_recv()
    v_sum = Sum(on_y, v_part, v_in, T // 2)

    def v_block(e):
        b = (4 - e) % 4
        rows = ag[b]
        text = dot(rows, wg[0].reshape(F, C), 1, 0)
        image = dot(rows, wg[1].reshape(F, C), 1, 0)
        part = jnp.where(image_rows(b, C), image, text)
        if e:
            v_part[e - 1] = part.astype(BF16)
        else:
            v_own[...] = part

    v_block(2)
    v_block(1)
    d_all.relay()
    v_sum.far()
    v_sum.near_up()
    v_block(3)
    v_sum.near_dn()
    v_block(0)
    d_all.finish()

    i_sum = Sum(on_z, i_part, i_in, 2 * T)

    def i_block(e):
        n = wrap(z + e)
        for b in range(4):
            rows = dv[b]
            text = dot(rows, wg[0, n], 1, 1)
            image = dot(rows, wg[1, n], 1, 1)
            part = jnp.where(image_rows(b, FB), image, text)
            if e:
                i_part[e - 1, b * T:(b + 1) * T] = part.astype(BF16)
            else:
                i_own[b * T:(b + 1) * T] = part

    i_block(2)
    i_sum.far()
    i_block(1)
    i_sum.near_up()
    i_block(3)
    i_sum.near_dn()
    i_block(0)

    feats = ag[...].reshape(4 * T, F)

    def update(kind):
        masked = [
            jnp.where(image_rows(b, C) == (kind == 1), dv[b].astype(F32), 0.0).astype(BF16) for b in range(4)
        ]
        return dot(feats, jnp.concatenate(masked, axis=0), 0, 0)

    w_other[...] = update(1 - c).astype(BF16)
    w_x = remote(w_other, w_recv, partner)
    v_sum.relay()
    i_sum.relay()
    w_own[...] = update(c)
    first, second = v_sum.finish(v_own)
    vg[0, 0:T // 2] = first.astype(BF16)
    vg[0, T // 2:T] = second.astype(BF16)
    v_all = gather(on_y, vg, T)
    v_all.start()

    w_x.wait_recv()
    w_sum = Sum(on_x, w_part, w_in, FB // 2)
    for e in (2, 1, 3, 0):
        rows = pl.ds(pl.multiple_of(wrap(x + e) * FB, FB), FB)
        summed = w_own[rows, :] + w_recv[rows, :].astype(F32)
        if e:
            w_part[e - 1] = summed.astype(BF16)
            (w_sum.near_up, w_sum.far, w_sum.near_dn)[e - 1]()
        else:
            w_mine[...] = summed
    v_all.relay()
    w_sum.relay()

    first, second = i_sum.finish(i_own)
    for b, rows in ((0, first[0:T]), (1, first[T:2 * T]), (2, second[0:T]), (3, second[T:2 * T])):
        igs[b] = rows.astype(BF16)
    cols = pl.ds(pl.multiple_of(z * FB, FB), FB)

    def last_move(b, action):
        n = wrap(y - b)
        copy = pltpu.make_async_remote_copy(
            src_ref=igs.at[b], dst_ref=igo.at[:, cols], send_sem=ssem_t.at[b], recv_sem=rsem_t.at[z],
            device_id=(c, n * 4 + x, y), device_id_type=MESH,
        )
        action(copy)

    for b in (1, 2, 3):
        last_move(b, lambda copy: copy.start())

    @pl.when(y != z)
    def _():
        last_move(0, lambda copy: copy.start())

    @pl.when(y == z)
    def _():
        igo[:, cols] = igs[0]

    v_all.finish()
    values = vg[...].reshape(4 * T, C)
    c_sum = Sum(on_x, c_part, c_in, T // 2)

    def c_block(e):
        a = (4 - e) % 4
        for h in range(NH):
            hs = slice(h * HD, (h + 1) * HD)
            part = dot(values[:, hs], pt[h, :, a * T:(a + 1) * T], 0, 0)
            part = (part * factor(a, h)).T
            if e:
                c_part[e - 1, :, hs] = part.astype(BF16)
            else:
                c_own[:, hs] = part

    c_block(2)
    c_sum.far()
    c_block(1)
    c_sum.near_up()
    c_block(3)
    c_sum.near_dn()
    c_block(0)

    first, second = w_sum.finish(w_mine)
    wo[c, 0:FB // 2] = first
    wo[c, FB // 2:FB] = second
    w_out = remote(wo.at[c], wo.at[c], partner)
    c_sum.relay()
    w_out.wait_recv()
    out_w = pltpu.make_async_copy(wo, wg_out, loc_sem.at[2])
    out_w.start()

    for n in range(4):

        @pl.when(jnp.logical_or(y != z, n != z))
        def _(n=n):
            pltpu.make_async_remote_copy(
                src_ref=igs.at[0], dst_ref=igo.at[:, n * FB:(n + 1) * FB], send_sem=ssem_t.at[0], recv_sem=rsem_t.at[n],
                device_id=(c, s, wrap(z + 1)), device_id_type=MESH,
            ).wait_recv()

    out_i = pltpu.make_async_copy(igo, ig_out, loc_sem.at[1])
    out_i.start()
    first, second = c_sum.finish(c_own)
    co[0:T // 2] = first.astype(BF16)
    co[T // 2:T] = second.astype(BF16)
    out_c = pltpu.make_async_copy(co, ctx_out, loc_sem.at[0])
    out_c.start()
    for copy in sends:
        copy.wait_send()
    for b in (1, 2, 3):
        last_move(b, lambda copy: copy.wait_send())

    @pl.when(y != z)
    def _():
        last_move(0, lambda copy: copy.wait_send())

    out_c.wait()
    out_i.wait()
    out_w.wait()


def shards(activations, modality, query_rows, key_rows, value_weight, context_grad):
    vm = lambda shape, dtype=BF16: pltpu.VMEM(shape, dtype)
    dma = lambda *shape: pltpu.SemaphoreType.DMA(shape)
    any_spec = pl.BlockSpec(memory_space=pl.ANY)
    ring_sum = lambda rows, cols: [vm((3, rows, cols)), vm((6, rows // 2, cols)), vm((rows, cols), F32)]
    ctx, ig, wgrad = pl.pallas_call(
        kernel,
        out_shape=(
            jax.ShapeDtypeStruct((T, C), BF16),
            jax.ShapeDtypeStruct((T, F), BF16),
            jax.ShapeDtypeStruct((2, T, C), F32),
        ),
        in_specs=[any_spec] * 6,
        out_specs=(any_spec,) * 3,
        scratch_shapes=[
            vm((1, T), jnp.int32), vm((4, 8, T), jnp.int32), vm((4, T, F)), vm((2, 4, FB, C)),
            vm((4, T, C)), vm((4, T, C)), vm((4, T, C)), vm((4, T, C)), vm((4, T, C)),
            vm((NH, 4 * T, 4 * T)), vm((4, 4, 8, T), F32), vm((4, NH, 8, T), F32), vm((4 * T, C)),
            *ring_sum(T, C), *ring_sum(T, C), *ring_sum(T, C), vm((T, C)),
            *ring_sum(4 * T, FB), vm((4, T, FB)), vm((T, F)),
            vm((F, C)), vm((F, C)), vm((F, C), F32), vm((FB, C), F32), vm((3, FB, C)), vm((6, FB // 2, C)), vm((2, FB, C), F32),
            dma(7), dma(2, 96), dma(4), dma(4),
        ],
        compiler_params=pltpu.CompilerParams(
            collective_id=0, has_side_effects=True, vmem_limit_bytes=60 * 2**20
        ),
        name="routed_attention",
    )(activations, modality, query_rows, key_rows, value_weight, context_grad)
    return ctx[None], ig[None], wgrad


def solution(mesh):
    return jax.shard_map(
        shards,
        mesh=mesh,
        in_specs=(
            P("dp", "sect", None),
            P("dp", "sect"),
            P("dp", "sect", "head"),
            P("dp", "sect", "head"),
            P(None, "sect", "head"),
            P("dp", "sect", "head"),
        ),
        out_specs=(P("dp", "sect", "head"), P("dp", "sect", "head"), P(None, "sect", "head")),
        check_vma=False,
    )
```

```python
import functools

import jax
import jax.numpy as jnp
from jax import lax
from jax.experimental import pallas as pl
from jax.experimental.pallas import tpu as pltpu
from jax.sharding import PartitionSpec as P

HD = 128
BLOCK = 128
EXP2_SCALE = HD ** (-0.5) * 1.4426950408889634
NEG = -1e30
MESH = pl.DeviceIdType.MESH
F32 = jnp.float32
BF16 = jnp.bfloat16

T = 256
C = 512
F = 1024
FB = 256
NH = C // HD
CH = C // 2


def dot(a, b, ca, cb):
    return lax.dot_general(a, b, (((ca,), (cb,)), ((), ())), preferred_element_type=F32)


def wrap(v):
    return lax.rem(v + 4, 4)


def kernel(
    act, mod, qin, kin, win, gin,
    ctx_out, ig_out, wg_out,
    mod_v, mg, ag, wg, qg, gg, kg, vg, dv,
    pt, st, fa, gs,
    d_part, d_in, d_own,
    v_part, v_in, v_own,
    c_part, c_in, c_own, co,
    i_part, i_in, i_own, igs, igo,
    w_other, w_recv, w_own, w_mine, w_part, w_in, wo,
    loc_sem, sems,
):
    c = lax.axis_index("dp")
    s = lax.axis_index("sect")
    z = lax.axis_index("head")
    y = s // 4
    x = lax.rem(s, 4)

    def on_x(d):
        return (c, y * 4 + wrap(x + d), z)

    def on_y(d):
        return (c, wrap(y + d) * 4 + x, z)

    def on_z(d):
        return (c, s, wrap(z + d))

    partner = (1 - c, s, z)
    copies, arrived = [], set()

    def remote(src, dst, dev):
        n = len(copies)
        copy = pltpu.make_async_remote_copy(
            src_ref=src, dst_ref=dst, send_sem=sems.at[0, n], recv_sem=sems.at[1, n],
            device_id=dev, device_id_type=MESH,
        )
        copies.append(copy)
        copy.start()
        return copy

    def need(*some):
        for copy in some:
            if id(copy) not in arrived:
                arrived.add(id(copy))
                copy.wait_recv()

    class Gather:
        def __init__(self, on, slot, own=None, fixed=False, after=()):
            self.on, self.slot, self.fixed, self.after = on, slot, fixed, after
            self.own = own or (lambda part: slot(0, part))
            self.far = []

        def there(self, d, part, step):
            return self.slot(d, part) if self.fixed else self.slot((d + step) % 4, part)

        def start(self):
            need(*self.after)
            a_up = remote(self.own(0), self.there(0, 0, 1), self.on(1))
            b_dn = remote(self.own(1), self.there(0, 1, -1), self.on(-1))
            b_up = remote(self.own(1), self.there(0, 1, 1), self.on(1))
            a_dn = remote(self.own(0), self.there(0, 0, -1), self.on(-1))
            self.near_1, self.near_3 = (a_up, b_up), (b_dn, a_dn)

        def ra(self):
            need(self.near_1[0])
            self.far.append(remote(self.slot(1, 0), self.there(1, 0, 1), self.on(1)))

        def rb(self):
            need(self.near_3[0])
            self.far.append(remote(self.slot(3, 1), self.there(3, 1, -1), self.on(-1)))

        def finish(self):
            need(*self.near_1, *self.near_3, *self.far)

    def gather(on, buf, u, own=None):
        cols = pl.ds(u * CH, CH)
        return Gather(on, lambda d, part: buf.at[d, pl.ds(part * (T // 2), T // 2), cols], own)

    class Sum:
        def __init__(self, on, part, inbox, own, half, cols):
            self.on, self.own, self.half, self.cols = on, own, half, pl.ds(*cols)
            self.part = lambda e, n: part.at[e - 1, pl.ds(n * half, half), self.cols]
            self.inbox = lambda n: inbox.at[n, :, self.cols]

        def far(self):
            self.f_up = remote(self.part(2, 0), self.inbox(0), self.on(1))
            self.f_dn = remote(self.part(2, 1), self.inbox(1), self.on(-1))

        def near_up(self):
            self.n_up = remote(self.part(1, 1), self.inbox(2), self.on(1))

        def near_dn(self):
            self.n_dn = remote(self.part(3, 0), self.inbox(3), self.on(-1))

        def ra(self):
            need(self.f_up)
            here = self.part(1, 0)
            here[...] = (here[...].astype(F32) + self.inbox(0)[...].astype(F32)).astype(BF16)
            self.s_up = remote(here, self.inbox(4), self.on(1))

        def rb(self):
            need(self.f_dn)
            here = self.part(3, 1)
            here[...] = (here[...].astype(F32) + self.inbox(1)[...].astype(F32)).astype(BF16)
            self.s_dn = remote(here, self.inbox(5), self.on(-1))

        def finish(self, out):
            need(self.n_up, self.n_dn, self.s_up, self.s_dn)
            for n, sources in enumerate(((4, 3), (2, 5))):
                rows = pl.ds(n * self.half, self.half)
                total = self.own[rows, self.cols]
                for source in sources:
                    total = total + self.inbox(source)[...].astype(F32)
                out[rows, self.cols] = total.astype(out.dtype)

    local = [
        pltpu.make_async_copy(mod, mod_v, loc_sem.at[0]),
        *(
            pltpu.make_async_copy(
                act.at[0, :, pl.ds(pl.multiple_of(n * F + x * FB, FB), FB)], ag.at[0, :, pl.ds(n * FB, FB)],
                loc_sem.at[7 + n],
            )
            for n in range(4)
        ),
        pltpu.make_async_copy(qin.at[0], qg.at[0], loc_sem.at[2]),
        pltpu.make_async_copy(kin.at[0], kg.at[0], loc_sem.at[3]),
        pltpu.make_async_copy(gin.at[0], gg.at[0], loc_sem.at[4]),
        pltpu.make_async_copy(win.at[0], wg.at[0, y], loc_sem.at[5]),
        pltpu.make_async_copy(win.at[1], wg.at[1, y], loc_sem.at[6]),
    ]
    for copy in local:
        copy.start()

    barrier = pltpu.get_barrier_semaphore()
    for d in (1, 2, 3):
        for dev in (on_x(d), on_y(d), on_z(d)):
            pl.semaphore_signal(barrier, inc=1, device_id=dev, device_id_type=MESH)
    pl.semaphore_signal(barrier, inc=1, device_id=partner, device_id_type=MESH)
    pl.semaphore_wait(barrier, 10)

    def hbm_half(ref, u):
        return lambda part: ref.at[0, pl.ds(part * (T // 2), T // 2), pl.ds(u * CH, CH)]

    q_all, k_all, g_all, d_all, v_all = (
        [gather(on, buf, u, None if src is None else hbm_half(src, u)) for u in range(2)]
        for on, buf, src in (
            (on_x, qg, qin), (on_y, kg, kin), (on_x, gg, gin), (on_x, dv, None), (on_y, vg, None)
        )
    )
    d_sum, v_sum, c_sum = (
        [Sum(on, part, inbox, own, T // 2, (u * CH, CH)) for u in range(2)]
        for on, part, inbox, own in (
            (on_y, d_part, d_in, d_own), (on_x, v_part, v_in, v_own), (on_x, c_part, c_in, c_own)
        )
    )
    i_sum = [Sum(on_z, i_part.at[b], i_in.at[b], i_own.at[b], T // 2, (0, FB)) for b in range(4)]
    w_sum = [Sum(on_y, w_part, w_in, w_mine, FB // 2, (u * CH, CH)) for u in range(2)]
    w_all = Gather(
        on_y, lambda d, part: wg.at[c, wrap(y - d), pl.ds(part * (FB // 2), FB // 2)],
        lambda part: win.at[c, pl.ds(part * (FB // 2), FB // 2)], fixed=True,
    )

    quarter = pl.ds(pl.multiple_of(z * (T // 4), T // 4), T // 4)
    a_x = []

    def spread():
        for d in (1, 3, 2):
            for n in range(4):
                theirs = pl.ds(pl.multiple_of(n * F + wrap(x + d) * FB, FB), FB)
                a_x.append(
                    remote(act.at[0, quarter, theirs], ag.at[d, quarter, pl.ds(n * FB, FB)], on_x(d))
                )

    def z_slot(d, part):
        first = pl.multiple_of(wrap(z - d) * (T // 4) + part * (T // 8), T // 8)
        return ag.at[pl.ds(1, 3), pl.ds(first, T // 8)]

    a_all = Gather(on_z, z_slot, fixed=True, after=a_x)

    ahead = lax.broadcasted_iota(jnp.int32, (T, T), 1) - lax.broadcasted_iota(jnp.int32, (T, T), 0)

    shut = [jnp.where(y >= b, 0.0, NEG) for b in range(4)]

    def scores(u, first, last):
        k_all[u].finish()
        q_all[u].finish()

        def block(a, _):
            p = wrap(x - a)
            cols = pl.ds(pl.multiple_of(a * T, T), T)
            for n in range(2):
                h = 2 * u + n
                hs = slice(h * HD, (h + 1) * HD)
                parts, tops = [], []
                for b in range(4):
                    sc = dot(kg[b, :, hs], qg[a, :, hs], 1, 1)
                    if b == 0:
                        sc = jnp.where(ahead >= (x - p) * T, sc, NEG)
                    parts.append(sc)
                    tops.append(jnp.max(sc, axis=0, keepdims=True) + shut[b])
                top = jnp.maximum(functools.reduce(jnp.maximum, tops), 0.1 * NEG)
                total = jnp.zeros((1, T), F32)
                for b in range(4):
                    pw = jnp.exp2(parts[b] * EXP2_SCALE - (top - shut[b]) * EXP2_SCALE)
                    total = total + jnp.sum(pw, axis=0, keepdims=True)
                    pt[h, b * T:(b + 1) * T, cols] = pw.astype(BF16)
                for m in range(2):
                    st[u, 0, p, 2 * n + m:2 * n + m + 1] = top[:, m * BLOCK:(m + 1) * BLOCK]
                    st[u, 0, p, 4 + 2 * n + m:5 + 2 * n + m] = total[:, m * BLOCK:(m + 1) * BLOCK]
            return 0

        lax.fori_loop(first, last, block, 0)

    st_x = [[], []]

    def send_stats(u):
        for d in (1, 3, 2):
            st_x[u].append(remote(st.at[u, 0], st.at[u, d], on_x(d)))

    def factor(a, h):
        return jnp.concatenate([fa[a, h]] * (HD // 8), axis=0)

    def scale(u):
        need(*st_x[u])
        g_all[u].finish()
        for a in range(4):
            p = wrap(x - a)
            tops = [st[u, d, p, 0:4] for d in range(4)]
            top = functools.reduce(jnp.maximum, tops)
            total = jnp.zeros_like(top)
            for d in range(4):
                total = total + st[u, d, p, 4:8] * jnp.exp2((tops[d] - top) * EXP2_SCALE)
            each = jnp.exp2((tops[0] - top) * EXP2_SCALE) / total
            for n in range(2):
                for m in range(2):
                    row = each[2 * n + m:2 * n + m + 1]
                    fa[a, 2 * u + n, :, m * BLOCK:(m + 1) * BLOCK] = jnp.broadcast_to(row, (8, BLOCK))
        for h in (2 * u, 2 * u + 1):
            hs = slice(h * HD, (h + 1) * HD)
            for a in range(4):
                wide = factor(a, h).T
                gs[a * T:(a + 1) * T, hs] = (gg[a, :, hs].astype(F32) * wide).astype(BF16)

    def d_block(u, e):
        b = (4 - e) % 4
        for h in (2 * u, 2 * u + 1):
            hs = slice(h * HD, (h + 1) * HD)
            part = dot(pt[h, b * T:(b + 1) * T, :], gs[:, hs], 1, 0)
            if e:
                d_part[e - 1, :, hs] = part.astype(BF16)
            else:
                d_own[:, hs] = part

    m_x, w_c = {}, {}

    def image_rows(b, width):
        if b:
            need(m_x[b])
        parts = []
        for n in range(T // BLOCK):
            tile = mg[b, :, n * BLOCK:(n + 1) * BLOCK]
            tile = jnp.concatenate([tile] * (width // BLOCK), axis=1)
            parts += [tile] * (BLOCK // 8)
        return jnp.concatenate(parts, axis=0) == 1

    def i_block(b, e):
        need(*w_c.values())
        for u in range(2):
            need(*((), d_all[u].near_1, d_all[u].far, d_all[u].near_3)[b])
        n = wrap(z + e)
        rows = dv[b]
        text = dot(rows, wg[0, n], 1, 1)
        image = dot(rows, wg[1, n], 1, 1)
        part = jnp.where(image_rows(b, FB), image, text)
        if e:
            i_part[b, e - 1] = part.astype(BF16)
        else:
            i_own[b] = part

    i_x = []

    def i_done(b):
        cols = pl.ds(pl.multiple_of(x * FB, FB), FB)
        if b:
            i_sum[b].finish(igs.at[b])
            i_x.append(remote(igs.at[b], igo.at[:, cols], on_x(-b)))
        else:
            i_sum[0].finish(igo.at[:, cols])

    def v_block(e):
        need(*w_c.values())
        a_all.finish()
        b = (4 - e) % 4
        rows = ag[b]
        text = dot(rows, wg[0].reshape(F, C), 1, 0)
        image = dot(rows, wg[1].reshape(F, C), 1, 0)
        part = jnp.where(image_rows(b, C), image, text)
        if e:
            v_part[e - 1] = part.astype(BF16)
        else:
            v_own[...] = part

    def update(kind, u):
        a_all.finish()
        d_all[u].finish()
        cols = slice(u * CH, (u + 1) * CH)
        masked = [
            jnp.where(image_rows(b, CH) == (kind == 1), dv[b, :, cols].astype(F32), 0.0).astype(BF16)
            for b in range(4)
        ]
        return dot(ag[...].reshape(4 * T, F), jnp.concatenate(masked, axis=0), 0, 0)

    def c_block(u, e):
        v_all[u].finish()
        a = (4 - e) % 4
        for h in (2 * u, 2 * u + 1):
            hs = slice(h * HD, (h + 1) * HD)
            values = vg[:, :, hs].reshape(4 * T, HD)
            part = dot(values, pt[h, :, a * T:(a + 1) * T], 0, 0)
            part = (part * factor(a, h)).T
            if e:
                c_part[e - 1, :, hs] = part.astype(BF16)
            else:
                c_own[:, hs] = part

    def d_done(u):
        d_sum[u].finish(dv.at[0])

    def v_done(u):
        v_sum[u].finish(vg.at[0])

    def c_done(u):
        c_sum[u].finish(co)

    def hand(d):
        need(*(w_all.near_1, w_all.far, w_all.near_3)[d - 1])
        block = wg.at[c, wrap(y - d)]
        w_c[d] = remote(block, block, partner)

    w_x, w_back = {}, []

    def w_other_kind(u):
        w_other[u] = update(1 - c, u).astype(BF16)
        w_x[u] = remote(w_other.at[u], w_recv.at[u], partner)

    def w_own_kind(u):
        w_own[u] = update(c, u)

    def w_add(u):
        need(w_x[u])
        cols = slice(u * CH, (u + 1) * CH)
        for e in range(4):
            rows = pl.ds(pl.multiple_of(wrap(y + e) * FB, FB), FB)
            summed = w_own[u, rows, :] + w_recv[u, rows, :].astype(F32)
            if e:
                w_part[e - 1, :, cols] = summed.astype(BF16)
            else:
                w_mine[:, cols] = summed

    def w_done(u):
        w_sum[u].finish(wo.at[c])
        block = wo.at[c, :, pl.ds(u * CH, CH)]
        w_back.append(remote(block, block, partner))

    spread()
    k_all[0].start()
    q_all[0].start()
    for copy in local:
        copy.wait()
    mg[0] = jnp.broadcast_to(mod_v[...], (8, T))
    for d in (1, 2, 3):
        m_x[d] = remote(mg.at[0], mg.at[d], on_x(d))
    k_all[0].ra()
    k_all[0].rb()
    k_all[1].start()
    k_all[1].ra()
    k_all[1].rb()
    w_all.start()
    a_all.start()
    q_all[0].ra()
    q_all[0].rb()
    q_all[1].start()
    scores(0, 0, 2)
    q_all[1].ra()
    q_all[1].rb()
    g_all[0].start()
    scores(0, 2, 4)
    send_stats(0)
    w_all.ra()
    w_all.rb()
    a_all.ra()
    a_all.rb()
    hand(1)
    hand(3)
    scores(1, 0, 2)
    g_all[0].ra()
    g_all[0].rb()
    g_all[1].start()
    scores(1, 2, 4)
    send_stats(1)
    hand(2)
    scale(0)
    d_block(0, 1)
    d_sum[0].near_up()
    v_block(2)
    g_all[1].ra()
    g_all[1].rb()
    v_sum[0].far()
    v_block(1)
    v_sum[0].near_up()
    v_block(3)
    v_sum[0].near_dn()
    v_block(0)
    v_sum[1].far()
    v_sum[1].near_dn()
    v_sum[1].near_up()
    d_block(0, 2)
    d_sum[0].far()
    d_block(0, 3)
    d_sum[0].near_dn()
    d_block(0, 0)
    scale(1)
    d_block(1, 1)
    d_sum[1].near_up()
    d_block(1, 2)
    d_sum[1].far()
    v_sum[0].ra()
    v_sum[0].rb()
    d_block(1, 3)
    d_sum[1].near_dn()
    d_sum[0].ra()
    d_sum[0].rb()
    d_block(1, 0)
    v_sum[1].ra()
    v_sum[1].rb()
    d_sum[1].rb()
    d_sum[1].ra()
    v_done(0)
    v_all[0].start()
    d_done(0)
    d_all[0].start()
    v_done(1)
    v_all[1].start()
    d_done(1)
    d_all[1].start()
    i_block(0, 2)
    i_sum[0].far()
    i_block(0, 1)
    i_sum[0].near_up()
    i_block(0, 3)
    i_sum[0].near_dn()
    i_block(0, 0)
    v_all[0].ra()
    v_all[0].rb()
    d_all[0].ra()
    d_all[0].rb()
    i_sum[0].ra()
    v_all[1].ra()
    v_all[1].rb()
    i_sum[0].rb()
    d_all[1].ra()
    d_all[1].rb()
    i_block(1, 2)
    i_sum[1].far()
    i_block(1, 1)
    i_sum[1].near_up()
    i_block(1, 3)
    i_sum[1].near_dn()
    i_block(1, 0)
    i_block(3, 2)
    i_sum[3].far()
    i_block(3, 1)
    i_sum[3].near_up()
    i_block(3, 3)
    i_sum[3].near_dn()
    i_done(0)
    i_block(3, 0)
    w_other_kind(0)
    i_block(2, 2)
    i_sum[2].far()
    i_block(2, 1)
    i_sum[1].ra()
    i_sum[1].rb()
    i_sum[2].near_up()
    i_block(2, 3)
    i_sum[2].near_dn()
    i_block(2, 0)
    w_own_kind(0)
    c_block(0, 2)
    c_sum[0].far()
    c_block(0, 1)
    c_sum[0].near_up()
    c_block(0, 3)
    c_sum[0].near_dn()
    c_block(0, 0)
    w_other_kind(1)
    i_sum[3].ra()
    i_sum[3].rb()
    w_add(0)
    w_own_kind(1)
    c_block(1, 2)
    c_sum[1].far()
    w_sum[0].far()
    w_sum[0].near_dn()
    w_sum[0].near_up()
    c_block(1, 1)
    c_sum[1].near_up()
    c_sum[0].ra()
    c_sum[0].rb()
    c_block(1, 3)
    c_sum[1].near_dn()
    c_block(1, 0)
    i_sum[2].ra()
    i_sum[2].rb()
    w_add(1)
    w_sum[1].far()
    i_done(1)
    w_sum[1].near_dn()
    w_sum[1].near_up()
    c_sum[1].ra()
    c_sum[1].rb()
    w_sum[0].ra()
    w_sum[0].rb()
    i_done(3)
    c_done(0)
    w_sum[1].ra()
    w_sum[1].rb()
    i_done(2)
    w_done(0)
    c_done(1)
    w_done(1)

    need(*i_x)
    out_i = pltpu.make_async_copy(igo, ig_out, loc_sem.at[1])
    out_i.start()
    need(*w_back)
    out_w = pltpu.make_async_copy(wo, wg_out, loc_sem.at[2])
    out_w.start()
    out_c = pltpu.make_async_copy(co, ctx_out, loc_sem.at[0])
    out_c.start()
    need(*copies)
    for copy in copies:
        copy.wait_send()
    out_c.wait()
    out_i.wait()
    out_w.wait()


def shards(activations, modality, query_rows, key_rows, value_weight, context_grad):
    vm = lambda shape, dtype=BF16: pltpu.VMEM(shape, dtype)
    dma = lambda *shape: pltpu.SemaphoreType.DMA(shape)
    any_spec = pl.BlockSpec(memory_space=pl.ANY)
    ring_sum = lambda rows, cols: [vm((3, rows, cols)), vm((6, rows // 2, cols)), vm((rows, cols), F32)]
    ctx, ig, wgrad = pl.pallas_call(
        kernel,
        out_shape=(
            jax.ShapeDtypeStruct((T, C), BF16),
            jax.ShapeDtypeStruct((T, F), BF16),
            jax.ShapeDtypeStruct((2, T, C), F32),
        ),
        in_specs=[any_spec] * 6,
        out_specs=(any_spec,) * 3,
        scratch_shapes=[
            vm((1, T), jnp.int32), vm((4, 8, T), jnp.int32), vm((4, T, F)), vm((2, 4, FB, C)),
            vm((4, T, C)), vm((4, T, C)), vm((4, T, C)), vm((4, T, C)), vm((4, T, C)),
            vm((NH, 4 * T, 4 * T)), vm((2, 4, 4, 8, BLOCK), F32), vm((4, NH, 8, T), F32), vm((4 * T, C)),
            *ring_sum(T, C), *ring_sum(T, C), *ring_sum(T, C), vm((T, C)),
            vm((4, 3, T, FB)), vm((4, 6, T // 2, FB)), vm((4, T, FB), F32), vm((4, T, FB)), vm((T, F)),
            vm((2, F, CH)), vm((2, F, CH)), vm((2, F, CH), F32), vm((FB, C), F32), vm((3, FB, C)), vm((6, FB // 2, C)), vm((2, FB, C), F32),
            dma(11), dma(2, 192),
        ],
        compiler_params=pltpu.CompilerParams(
            collective_id=0, has_side_effects=True, vmem_limit_bytes=60 * 2**20
        ),
        name="routed_attention",
    )(activations, modality, query_rows, key_rows, value_weight, context_grad)
    return tuple(hand_out(ctx[None], ig[None], wgrad))


def hand_out_kernel(*refs):
    sem = refs[-1]
    moves = []
    for src, buf, dst in zip(refs[:3], refs[6:9], refs[3:6]):
        for n in range(src.shape[0]):
            for m in range(2):
                rows = pl.ds(m * 128, 128)
                k = len(moves)
                moves.append((
                    pltpu.make_async_copy(src.at[n, rows], buf.at[n, rows], sem.at[0, k]),
                    pltpu.make_async_copy(buf.at[n, rows], dst.at[n, rows], sem.at[1, k]),
                ))
    for come, _ in moves:
        come.start()
    for come, go in moves:
        come.wait()
        go.start()
    for _, go in moves:
        go.wait()


def hand_out(*arrays):
    any_spec = pl.BlockSpec(memory_space=pl.ANY)
    return pl.pallas_call(
        hand_out_kernel,
        out_shape=tuple(jax.ShapeDtypeStruct(a.shape, a.dtype) for a in arrays),
        in_specs=[any_spec] * 3,
        out_specs=(any_spec,) * 3,
        scratch_shapes=[*(pltpu.VMEM(a.shape, a.dtype) for a in arrays), pltpu.SemaphoreType.DMA((2, 8))],
        name="hand_out",
    )(*arrays)


def solution(mesh):
    return jax.shard_map(
        shards,
        mesh=mesh,
        in_specs=(
            P("dp", "sect", None),
            P("dp", "sect"),
            P("dp", "sect", "head"),
            P("dp", "sect", "head"),
            P(None, "sect", "head"),
            P("dp", "sect", "head"),
        ),
        out_specs=(P("dp", "sect", "head"), P("dp", "sect", "head"), P(None, "sect", "head")),
        check_vma=False,
    )
```

```python
import functools

import jax
import jax.numpy as jnp
from jax import lax
from jax.experimental import pallas as pl
from jax.experimental.pallas import tpu as pltpu
from jax.sharding import PartitionSpec as P

HD = 128
BLOCK = 128
EXP2_SCALE = HD ** (-0.5) * 1.4426950408889634
NEG = -1e30
MESH = pl.DeviceIdType.MESH
F32 = jnp.float32
BF16 = jnp.bfloat16

T = 256
C = 512
F = 1024
FB = 256
NH = C // HD
CH = C // 2


def dot(a, b, ca, cb):
    return lax.dot_general(a, b, (((ca,), (cb,)), ((), ())), preferred_element_type=F32)


def wrap(v):
    return lax.rem(v + 4, 4)


def kernel(
    act, mod, qin, kin, win, gin,
    ctx_out, ig_out, wg_out,
    mod_v, mg, ag, wg, qg, gg, kg, vg, dv,
    pt, st, fa, gs,
    d_part, d_in, d_own,
    v_part, v_in, v_own,
    c_part, c_in, c_own, co,
    i_part, i_in, i_own, igs, igo,
    w_other, w_recv, w_own, w_mine, w_part, w_in, wo,
    loc_sem, sems,
):
    c = lax.axis_index("dp")
    s = lax.axis_index("sect")
    z = lax.axis_index("head")
    y = s // 4
    x = lax.rem(s, 4)

    def on_x(d):
        return (c, y * 4 + wrap(x + d), z)

    def on_y(d):
        return (c, wrap(y + d) * 4 + x, z)

    def on_z(d):
        return (c, s, wrap(z + d))

    partner = (1 - c, s, z)
    copies, arrived = [], set()

    def remote(src, dst, dev):
        n = len(copies)
        copy = pltpu.make_async_remote_copy(
            src_ref=src, dst_ref=dst, send_sem=sems.at[0, n], recv_sem=sems.at[1, n],
            device_id=dev, device_id_type=MESH,
        )
        copies.append(copy)
        copy.start()
        return copy

    def need(*some):
        for copy in some:
            if id(copy) not in arrived:
                arrived.add(id(copy))
                copy.wait_recv()

    class Gather:
        def __init__(self, on, slot, own=None, fixed=False, after=()):
            self.on, self.slot, self.fixed, self.after = on, slot, fixed, after
            self.own = own or (lambda part: slot(0, part))
            self.far = []

        def there(self, d, part, step):
            return self.slot(d, part) if self.fixed else self.slot((d + step) % 4, part)

        def start(self):
            need(*self.after)
            a_up = remote(self.own(0), self.there(0, 0, 1), self.on(1))
            b_dn = remote(self.own(1), self.there(0, 1, -1), self.on(-1))
            b_up = remote(self.own(1), self.there(0, 1, 1), self.on(1))
            a_dn = remote(self.own(0), self.there(0, 0, -1), self.on(-1))
            self.near_1, self.near_3 = (a_up, b_up), (b_dn, a_dn)

        def ra(self):
            need(self.near_1[0])
            self.far.append(remote(self.slot(1, 0), self.there(1, 0, 1), self.on(1)))

        def rb(self):
            need(self.near_3[0])
            self.far.append(remote(self.slot(3, 1), self.there(3, 1, -1), self.on(-1)))

        def finish(self):
            need(*self.near_1, *self.near_3, *self.far)

    def gather(on, buf, u, own=None):
        cols = pl.ds(u * CH, CH)
        return Gather(on, lambda d, part: buf.at[d, pl.ds(part * (T // 2), T // 2), cols], own)

    class Sum:
        def __init__(self, on, part, inbox, own, half, cols):
            self.on, self.own, self.half, self.cols = on, own, half, pl.ds(*cols)
            self.part = lambda e, n: part.at[e - 1, pl.ds(n * half, half), self.cols]
            self.inbox = lambda n: inbox.at[n, :, self.cols]

        def far(self):
            self.f_up = remote(self.part(2, 0), self.inbox(0), self.on(1))
            self.f_dn = remote(self.part(2, 1), self.inbox(1), self.on(-1))

        def near_up(self):
            self.n_up = remote(self.part(1, 1), self.inbox(2), self.on(1))

        def near_dn(self):
            self.n_dn = remote(self.part(3, 0), self.inbox(3), self.on(-1))

        def ra(self):
            need(self.f_up)
            here = self.part(1, 0)
            here[...] = (here[...].astype(F32) + self.inbox(0)[...].astype(F32)).astype(BF16)
            self.s_up = remote(here, self.inbox(4), self.on(1))

        def rb(self):
            need(self.f_dn)
            here = self.part(3, 1)
            here[...] = (here[...].astype(F32) + self.inbox(1)[...].astype(F32)).astype(BF16)
            self.s_dn = remote(here, self.inbox(5), self.on(-1))

        def finish(self, out):
            need(self.n_up, self.n_dn, self.s_up, self.s_dn)
            for n, sources in enumerate(((4, 3), (2, 5))):
                rows = pl.ds(n * self.half, self.half)
                total = self.own[rows, self.cols]
                for source in sources:
                    total = total + self.inbox(source)[...].astype(F32)
                out[rows, self.cols] = total.astype(out.dtype)

    local = [
        pltpu.make_async_copy(mod, mod_v, loc_sem.at[0]),
        *(
            pltpu.make_async_copy(
                act.at[0, :, pl.ds(pl.multiple_of(n * F + x * FB, FB), FB)], ag.at[0, :, pl.ds(n * FB, FB)],
                loc_sem.at[7 + n],
            )
            for n in range(4)
        ),
        pltpu.make_async_copy(qin.at[0], qg.at[0], loc_sem.at[2]),
        pltpu.make_async_copy(kin.at[0], kg.at[0], loc_sem.at[3]),
        pltpu.make_async_copy(gin.at[0], gg.at[0], loc_sem.at[4]),
        pltpu.make_async_copy(win.at[0], wg.at[0, y], loc_sem.at[5]),
        pltpu.make_async_copy(win.at[1], wg.at[1, y], loc_sem.at[6]),
    ]
    for copy in local:
        copy.start()

    barrier = pltpu.get_barrier_semaphore()
    for d in (1, 2, 3):
        for dev in (on_x(d), on_y(d), on_z(d)):
            pl.semaphore_signal(barrier, inc=1, device_id=dev, device_id_type=MESH)
    pl.semaphore_signal(barrier, inc=1, device_id=partner, device_id_type=MESH)
    pl.semaphore_wait(barrier, 10)

    def hbm_half(ref, u):
        return lambda part: ref.at[0, pl.ds(part * (T // 2), T // 2), pl.ds(u * CH, CH)]

    q_all, k_all, g_all, d_all, v_all = (
        [gather(on, buf, u, None if src is None else hbm_half(src, u)) for u in range(2)]
        for on, buf, src in (
            (on_x, qg, qin), (on_y, kg, kin), (on_x, gg, gin), (on_x, dv, None), (on_y, vg, None)
        )
    )
    d_sum, v_sum, c_sum = (
        [Sum(on, part, inbox, own, T // 2, (u * CH, CH)) for u in range(2)]
        for on, part, inbox, own in (
            (on_y, d_part, d_in, d_own), (on_x, v_part, v_in, v_own), (on_x, c_part, c_in, c_own)
        )
    )
    i_sum = [Sum(on_z, i_part.at[b], i_in.at[b], i_own.at[b], T // 2, (0, FB)) for b in range(4)]
    w_sum = [Sum(on_y, w_part, w_in, w_mine, FB // 2, (u * CH, CH)) for u in range(2)]
    w_all = Gather(
        on_y, lambda d, part: wg.at[c, wrap(y - d), pl.ds(part * (FB // 2), FB // 2)],
        lambda part: win.at[c, pl.ds(part * (FB // 2), FB // 2)], fixed=True,
    )

    quarter = pl.ds(pl.multiple_of(z * (T // 4), T // 4), T // 4)
    a_x = []

    def spread():
        for d in (1, 3, 2):
            for n in range(4):
                theirs = pl.ds(pl.multiple_of(n * F + wrap(x + d) * FB, FB), FB)
                a_x.append(
                    remote(act.at[0, quarter, theirs], ag.at[d, quarter, pl.ds(n * FB, FB)], on_x(d))
                )

    def z_slot(d, part):
        first = pl.multiple_of(wrap(z - d) * (T // 4) + part * (T // 8), T // 8)
        return ag.at[pl.ds(1, 3), pl.ds(first, T // 8)]

    a_all = Gather(on_z, z_slot, fixed=True, after=a_x)

    ahead = lax.broadcasted_iota(jnp.int32, (T, T), 1) - lax.broadcasted_iota(jnp.int32, (T, T), 0)

    shut = [jnp.where(y >= b, 0.0, NEG) for b in range(4)]

    def scores(u, first, last):
        k_all[u].finish()
        q_all[u].finish()

        def block(a, _):
            p = wrap(x - a)
            cols = pl.ds(pl.multiple_of(a * T, T), T)
            for n in range(2):
                h = 2 * u + n
                hs = slice(h * HD, (h + 1) * HD)
                parts, tops = [], []
                for b in range(4):
                    sc = dot(kg[b, :, hs], qg[a, :, hs], 1, 1)
                    if b == 0:
                        sc = jnp.where(ahead >= (x - p) * T, sc, NEG)
                    parts.append(sc)
                    tops.append(jnp.max(sc, axis=0, keepdims=True) + shut[b])
                top = jnp.maximum(functools.reduce(jnp.maximum, tops), 0.1 * NEG)
                total = jnp.zeros((1, T), F32)
                for b in range(4):
                    pw = jnp.exp2(parts[b] * EXP2_SCALE - (top - shut[b]) * EXP2_SCALE)
                    total = total + jnp.sum(pw, axis=0, keepdims=True)
                    pt[h, b * T:(b + 1) * T, cols] = pw.astype(BF16)
                for m in range(2):
                    st[u, 0, p, 2 * n + m:2 * n + m + 1] = top[:, m * BLOCK:(m + 1) * BLOCK]
                    st[u, 0, p, 4 + 2 * n + m:5 + 2 * n + m] = total[:, m * BLOCK:(m + 1) * BLOCK]
            return 0

        lax.fori_loop(first, last, block, 0)

    st_x = [[], []]

    def send_stats(u):
        for d in (1, 3, 2):
            st_x[u].append(remote(st.at[u, 0], st.at[u, d], on_x(d)))

    def factor(a, h):
        return jnp.concatenate([fa[a, h]] * (HD // 8), axis=0)

    def scale(u):
        need(*st_x[u])
        g_all[u].finish()
        for a in range(4):
            p = wrap(x - a)
            tops = [st[u, d, p, 0:4] for d in range(4)]
            top = functools.reduce(jnp.maximum, tops)
            total = jnp.zeros_like(top)
            for d in range(4):
                total = total + st[u, d, p, 4:8] * jnp.exp2((tops[d] - top) * EXP2_SCALE)
            each = jnp.exp2((tops[0] - top) * EXP2_SCALE) / total
            for n in range(2):
                for m in range(2):
                    row = each[2 * n + m:2 * n + m + 1]
                    fa[a, 2 * u + n, :, m * BLOCK:(m + 1) * BLOCK] = jnp.broadcast_to(row, (8, BLOCK))
        for h in (2 * u, 2 * u + 1):
            hs = slice(h * HD, (h + 1) * HD)
            for a in range(4):
                wide = factor(a, h).T
                gs[a * T:(a + 1) * T, hs] = (gg[a, :, hs].astype(F32) * wide).astype(BF16)

    def d_block(u, e):
        b = (4 - e) % 4
        for h in (2 * u, 2 * u + 1):
            hs = slice(h * HD, (h + 1) * HD)
            part = dot(pt[h, b * T:(b + 1) * T, :], gs[:, hs], 1, 0)
            if e:
                d_part[e - 1, :, hs] = part.astype(BF16)
            else:
                d_own[:, hs] = part

    m_x, w_c = {}, {}

    def image_rows(b, width):
        if b:
            need(m_x[b])
        parts = []
        for n in range(T // BLOCK):
            tile = mg[b, :, n * BLOCK:(n + 1) * BLOCK]
            tile = jnp.concatenate([tile] * (width // BLOCK), axis=1)
            parts += [tile] * (BLOCK // 8)
        return jnp.concatenate(parts, axis=0) == 1

    def i_block(b, e):
        need(*w_c.values())
        for u in range(2):
            if b:
                need(*(d_all[u].near_1, d_all[u].far, d_all[u].near_3)[b - 1])
        n = wrap(z + e)
        rows = dv[b]
        text = dot(rows, wg[0, n], 1, 1)
        image = dot(rows, wg[1, n], 1, 1)
        part = jnp.where(image_rows(b, FB), image, text)
        if e:
            i_part[b, e - 1] = part.astype(BF16)
        else:
            i_own[b] = part

    i_x = []

    def i_done(b):
        cols = pl.ds(pl.multiple_of(x * FB, FB), FB)
        if b:
            i_sum[b].finish(igs.at[b])
            i_x.append(remote(igs.at[b], igo.at[:, cols], on_x(-b)))
        else:
            i_sum[0].finish(igo.at[:, cols])

    def v_block(e):
        need(*w_c.values())
        a_all.finish()
        b = (4 - e) % 4
        rows = ag[b]
        text = dot(rows, wg[0].reshape(F, C), 1, 0)
        image = dot(rows, wg[1].reshape(F, C), 1, 0)
        part = jnp.where(image_rows(b, C), image, text)
        if e:
            v_part[e - 1] = part.astype(BF16)
        else:
            v_own[...] = part

    def update(kind, u):
        a_all.finish()
        d_all[u].finish()
        cols = slice(u * CH, (u + 1) * CH)
        masked = [
            jnp.where(image_rows(b, CH) == (kind == 1), dv[b, :, cols].astype(F32), 0.0).astype(BF16)
            for b in range(4)
        ]
        return dot(ag[...].reshape(4 * T, F), jnp.concatenate(masked, axis=0), 0, 0)

    def c_block(u, e):
        v_all[u].finish()
        a = (4 - e) % 4
        for h in (2 * u, 2 * u + 1):
            hs = slice(h * HD, (h + 1) * HD)
            values = vg[:, :, hs].reshape(4 * T, HD)
            part = dot(values, pt[h, :, a * T:(a + 1) * T], 0, 0)
            part = (part * factor(a, h)).T
            if e:
                c_part[e - 1, :, hs] = part.astype(BF16)
            else:
                c_own[:, hs] = part

    def d_done(u):
        d_sum[u].finish(dv.at[0])

    def v_done(u):
        v_sum[u].finish(vg.at[0])

    def c_done(u):
        c_sum[u].finish(co)

    def hand(d):
        need(*(w_all.near_1, w_all.far, w_all.near_3)[d - 1])
        block = wg.at[c, wrap(y - d)]
        w_c[d] = remote(block, block, partner)

    w_x, w_back = {}, []

    def w_other_kind(u):
        w_other[u] = update(1 - c, u).astype(BF16)
        w_x[u] = remote(w_other.at[u], w_recv.at[u], partner)

    def w_own_kind(u):
        w_own[u] = update(c, u)

    def w_add(u):
        need(w_x[u])
        cols = slice(u * CH, (u + 1) * CH)
        for e in range(4):
            rows = pl.ds(pl.multiple_of(wrap(y + e) * FB, FB), FB)
            summed = w_own[u, rows, :] + w_recv[u, rows, :].astype(F32)
            if e:
                w_part[e - 1, :, cols] = summed.astype(BF16)
            else:
                w_mine[:, cols] = summed

    def w_done(u):
        w_sum[u].finish(wo.at[c])
        block = wo.at[c, :, pl.ds(u * CH, CH)]
        w_back.append(remote(block, block, partner))

    q_all[0].start()
    k_all[0].start()
    spread()
    for copy in local:
        copy.wait()
    mg[0] = jnp.broadcast_to(mod_v[...], (8, T))
    for d in (1, 2, 3):
        m_x[d] = remote(mg.at[0], mg.at[d], on_x(d))
    q_all[0].ra()
    q_all[0].rb()
    k_all[0].ra()
    q_all[1].start()
    k_all[0].rb()
    k_all[1].start()
    k_all[1].ra()
    k_all[1].rb()
    w_all.start()
    a_all.start()
    scores(0, 0, 2)
    q_all[1].ra()
    q_all[1].rb()
    g_all[0].start()
    scores(0, 2, 4)
    send_stats(0)
    w_all.ra()
    w_all.rb()
    scores(1, 0, 2)
    g_all[0].rb()
    g_all[0].ra()
    g_all[1].start()
    a_all.rb()
    hand(1)
    hand(3)
    a_all.ra()
    scores(1, 2, 4)
    send_stats(1)
    hand(2)
    scale(0)
    d_block(0, 1)
    d_block(0, 2)
    g_all[1].rb()
    g_all[1].ra()
    d_block(0, 0)
    d_sum[0].far()
    d_sum[0].near_up()
    d_block(0, 3)
    d_sum[0].near_dn()
    v_block(2)
    v_sum[1].far()
    v_sum[0].far()
    v_block(3)
    v_sum[0].near_dn()
    scale(1)
    d_block(1, 2)
    d_sum[1].far()
    d_block(1, 1)
    d_sum[1].near_up()
    d_block(1, 3)
    d_sum[1].near_dn()
    v_block(1)
    v_sum[1].near_up()
    v_block(0)
    v_sum[1].ra()
    d_block(1, 0)
    v_sum[1].near_dn()
    v_sum[1].rb()
    v_sum[0].near_up()
    d_sum[0].rb()
    d_sum[0].ra()
    v_sum[0].ra()
    v_sum[0].rb()
    d_sum[1].ra()
    d_sum[1].rb()
    d_done(0)
    d_all[0].start()
    v_done(1)
    v_all[1].start()
    d_done(1)
    d_all[1].start()
    i_block(0, 2)
    i_sum[0].far()
    i_block(0, 1)
    i_sum[0].near_up()
    v_done(0)
    v_all[0].start()
    i_block(0, 3)
    i_sum[0].near_dn()
    i_block(0, 0)
    d_all[0].ra()
    d_all[0].rb()
    v_all[1].ra()
    v_all[1].rb()
    i_sum[0].ra()
    i_sum[0].rb()
    d_all[1].ra()
    d_all[1].rb()
    v_all[0].ra()
    v_all[0].rb()
    i_block(3, 1)
    i_sum[3].near_up()
    i_block(3, 3)
    i_block(3, 0)
    i_block(1, 2)
    i_sum[1].far()
    i_block(1, 3)
    i_block(1, 1)
    i_sum[1].near_up()
    i_sum[1].near_dn()
    w_other_kind(0)
    w_own_kind(0)
    i_block(2, 2)
    i_sum[2].far()
    i_block(2, 1)
    i_sum[2].near_up()
    i_block(2, 3)
    i_sum[2].near_dn()
    c_block(0, 2)
    c_sum[0].far()
    w_other_kind(1)
    c_block(1, 3)
    c_sum[1].near_dn()
    i_sum[1].ra()
    c_block(1, 2)
    c_sum[1].far()
    c_block(1, 0)
    i_block(3, 2)
    i_sum[3].far()
    w_add(0)
    w_sum[0].far()
    w_sum[0].near_dn()
    w_sum[0].near_up()
    c_block(0, 1)
    c_sum[0].near_up()
    c_block(0, 3)
    c_sum[0].near_dn()
    i_sum[3].near_dn()
    c_block(0, 0)
    i_sum[2].rb()
    c_sum[0].ra()
    c_sum[0].rb()
    i_block(1, 0)
    i_sum[2].ra()
    i_done(0)
    i_sum[1].rb()
    w_own_kind(1)
    w_add(1)
    w_sum[1].near_dn()
    w_sum[1].near_up()
    w_sum[1].far()
    i_block(2, 0)
    c_block(1, 1)
    c_sum[1].near_up()
    c_sum[1].ra()
    w_sum[0].rb()
    w_sum[0].ra()
    i_sum[3].rb()
    c_sum[1].rb()
    i_sum[3].ra()
    c_done(0)
    i_done(2)
    w_sum[1].ra()
    w_sum[1].rb()
    i_done(1)
    c_done(1)
    w_done(0)
    i_done(3)
    w_done(1)

    need(*i_x)
    out_i = pltpu.make_async_copy(igo, ig_out, loc_sem.at[1])
    out_i.start()
    need(*w_back)
    out_w = pltpu.make_async_copy(wo, wg_out, loc_sem.at[2])
    out_w.start()
    out_c = pltpu.make_async_copy(co, ctx_out, loc_sem.at[0])
    out_c.start()
    need(*copies)
    for copy in copies:
        copy.wait_send()
    out_c.wait()
    out_i.wait()
    out_w.wait()


def shards(activations, modality, query_rows, key_rows, value_weight, context_grad):
    vm = lambda shape, dtype=BF16: pltpu.VMEM(shape, dtype)
    dma = lambda *shape: pltpu.SemaphoreType.DMA(shape)
    any_spec = pl.BlockSpec(memory_space=pl.ANY)
    ring_sum = lambda rows, cols: [vm((3, rows, cols)), vm((6, rows // 2, cols)), vm((rows, cols), F32)]
    ctx, ig, wgrad = pl.pallas_call(
        kernel,
        out_shape=(
            jax.ShapeDtypeStruct((T, C), BF16),
            jax.ShapeDtypeStruct((T, F), BF16),
            jax.ShapeDtypeStruct((2, T, C), F32),
        ),
        in_specs=[any_spec] * 6,
        out_specs=(any_spec,) * 3,
        scratch_shapes=[
            vm((1, T), jnp.int32), vm((4, 8, T), jnp.int32), vm((4, T, F)), vm((2, 4, FB, C)),
            vm((4, T, C)), vm((4, T, C)), vm((4, T, C)), vm((4, T, C)), vm((4, T, C)),
            vm((NH, 4 * T, 4 * T)), vm((2, 4, 4, 8, BLOCK), F32), vm((4, NH, 8, T), F32), vm((4 * T, C)),
            *ring_sum(T, C), *ring_sum(T, C), *ring_sum(T, C), vm((T, C)),
            vm((4, 3, T, FB)), vm((4, 6, T // 2, FB)), vm((4, T, FB), F32), vm((4, T, FB)), vm((T, F)),
            vm((2, F, CH)), vm((2, F, CH)), vm((2, F, CH), F32), vm((FB, C), F32), vm((3, FB, C)), vm((6, FB // 2, C)), vm((2, FB, C), F32),
            dma(11), dma(2, 192),
        ],
        compiler_params=pltpu.CompilerParams(
            collective_id=0, has_side_effects=True, vmem_limit_bytes=60 * 2**20
        ),
        name="routed_attention",
    )(activations, modality, query_rows, key_rows, value_weight, context_grad)
    return tuple(hand_out(ctx[None], ig[None], wgrad))


def hand_out_kernel(*refs):
    sem = refs[-1]
    moves = []
    for src, buf, dst in zip(refs[:3], refs[6:9], refs[3:6]):
        for n in range(src.shape[0]):
            for m in range(2):
                rows = pl.ds(m * 128, 128)
                k = len(moves)
                moves.append((
                    pltpu.make_async_copy(src.at[n, rows], buf.at[n, rows], sem.at[0, k]),
                    pltpu.make_async_copy(buf.at[n, rows], dst.at[n, rows], sem.at[1, k]),
                ))
    for come, _ in moves:
        come.start()
    for come, go in moves:
        come.wait()
        go.start()
    for _, go in moves:
        go.wait()


def hand_out(*arrays):
    any_spec = pl.BlockSpec(memory_space=pl.ANY)
    return pl.pallas_call(
        hand_out_kernel,
        out_shape=tuple(jax.ShapeDtypeStruct(a.shape, a.dtype) for a in arrays),
        in_specs=[any_spec] * 3,
        out_specs=(any_spec,) * 3,
        scratch_shapes=[*(pltpu.VMEM(a.shape, a.dtype) for a in arrays), pltpu.SemaphoreType.DMA((2, 8))],
        name="hand_out",
    )(*arrays)


def solution(mesh):
    return jax.shard_map(
        shards,
        mesh=mesh,
        in_specs=(
            P("dp", "sect", None),
            P("dp", "sect"),
            P("dp", "sect", "head"),
            P("dp", "sect", "head"),
            P(None, "sect", "head"),
            P("dp", "sect", "head"),
        ),
        out_specs=(P("dp", "sect", "head"), P("dp", "sect", "head"), P(None, "sect", "head")),
        check_vma=False,
    )
```

```python
import functools

import jax
import jax.numpy as jnp
from jax import lax
from jax.experimental import pallas as pl
from jax.experimental.pallas import tpu as pltpu
from jax.sharding import PartitionSpec as P

HD = 128
BLOCK = 128
EXP2_SCALE = HD ** (-0.5) * 1.4426950408889634
NEG = -1e30
MESH = pl.DeviceIdType.MESH
F32 = jnp.float32
BF16 = jnp.bfloat16

T = 256
C = 512
F = 1024
FB = 256
NH = C // HD
CH = C // 2


def dot(a, b, ca, cb):
    return lax.dot_general(a, b, (((ca,), (cb,)), ((), ())), preferred_element_type=F32)


def wrap(v):
    return lax.rem(v + 4, 4)


def kernel(
    act, mod, qin, kin, win, gin,
    ctx_out, ig_out, wg_out,
    mod_v, mg, ag, wg, qg, gg, kg, vg, dv,
    pt, st, fa, gs,
    d_part, d_in, d_own,
    v_part, v_in, v_own,
    c_part, c_in, c_own, co,
    i_part, i_in, i_own, igs, igo,
    w_other, w_recv, w_own, w_mine, w_part, w_in, wo,
    loc_sem, sems,
):
    c = lax.axis_index("dp")
    s = lax.axis_index("sect")
    z = lax.axis_index("head")
    y = s // 4
    x = lax.rem(s, 4)

    def on_x(d):
        return (c, y * 4 + wrap(x + d), z)

    def on_y(d):
        return (c, wrap(y + d) * 4 + x, z)

    def on_z(d):
        return (c, s, wrap(z + d))

    partner = (1 - c, s, z)
    copies, arrived = [], set()

    def remote(src, dst, dev):
        n = len(copies)
        copy = pltpu.make_async_remote_copy(
            src_ref=src, dst_ref=dst, send_sem=sems.at[0, n], recv_sem=sems.at[1, n],
            device_id=dev, device_id_type=MESH,
        )
        copies.append(copy)
        copy.start()
        return copy

    def need(*some):
        for copy in some:
            if id(copy) not in arrived:
                arrived.add(id(copy))
                copy.wait_recv()

    class Gather:
        def __init__(self, on, slot, own=None, fixed=False, after=()):
            self.on, self.slot, self.fixed, self.after = on, slot, fixed, after
            self.own = own or (lambda part: slot(0, part))
            self.far = []

        def there(self, d, part, step):
            return self.slot(d, part) if self.fixed else self.slot((d + step) % 4, part)

        def start(self):
            need(*self.after)
            a_up = remote(self.own(0), self.there(0, 0, 1), self.on(1))
            b_dn = remote(self.own(1), self.there(0, 1, -1), self.on(-1))
            b_up = remote(self.own(1), self.there(0, 1, 1), self.on(1))
            a_dn = remote(self.own(0), self.there(0, 0, -1), self.on(-1))
            self.near_1, self.near_3 = (a_up, b_up), (b_dn, a_dn)

        def ra(self):
            need(self.near_1[0])
            self.far.append(remote(self.slot(1, 0), self.there(1, 0, 1), self.on(1)))

        def rb(self):
            need(self.near_3[0])
            self.far.append(remote(self.slot(3, 1), self.there(3, 1, -1), self.on(-1)))

        def finish(self):
            need(*self.near_1, *self.near_3, *self.far)

    def gather(on, buf, u, own=None):
        cols = pl.ds(u * CH, CH)
        return Gather(on, lambda d, part: buf.at[d, pl.ds(part * (T // 2), T // 2), cols], own)

    class Sum:
        def __init__(self, on, part, inbox, own, half, cols):
            self.on, self.own, self.half, self.cols = on, own, half, pl.ds(*cols)
            self.part = lambda e, n: part.at[e - 1, pl.ds(n * half, half), self.cols]
            self.inbox = lambda n: inbox.at[n, :, self.cols]

        def far(self):
            self.f_up = remote(self.part(2, 0), self.inbox(0), self.on(1))
            self.f_dn = remote(self.part(2, 1), self.inbox(1), self.on(-1))

        def near_up(self):
            self.n_up = remote(self.part(1, 1), self.inbox(2), self.on(1))

        def near_dn(self):
            self.n_dn = remote(self.part(3, 0), self.inbox(3), self.on(-1))

        def ra(self):
            need(self.f_up)
            here = self.part(1, 0)
            here[...] = (here[...].astype(F32) + self.inbox(0)[...].astype(F32)).astype(BF16)
            self.s_up = remote(here, self.inbox(4), self.on(1))

        def rb(self):
            need(self.f_dn)
            here = self.part(3, 1)
            here[...] = (here[...].astype(F32) + self.inbox(1)[...].astype(F32)).astype(BF16)
            self.s_dn = remote(here, self.inbox(5), self.on(-1))

        def finish(self, out):
            need(self.n_up, self.n_dn, self.s_up, self.s_dn)
            for n, sources in enumerate(((4, 3), (2, 5))):
                rows = pl.ds(n * self.half, self.half)
                total = self.own[rows, self.cols]
                for source in sources:
                    total = total + self.inbox(source)[...].astype(F32)
                out[rows, self.cols] = total.astype(out.dtype)

    local = [
        pltpu.make_async_copy(mod, mod_v, loc_sem.at[0]),
        *(
            pltpu.make_async_copy(
                act.at[0, :, pl.ds(pl.multiple_of(n * F + x * FB, FB), FB)], ag.at[0, :, pl.ds(n * FB, FB)],
                loc_sem.at[7 + n],
            )
            for n in range(4)
        ),
        pltpu.make_async_copy(qin.at[0], qg.at[0], loc_sem.at[2]),
        pltpu.make_async_copy(kin.at[0], kg.at[0], loc_sem.at[3]),
        pltpu.make_async_copy(gin.at[0], gg.at[0], loc_sem.at[4]),
        pltpu.make_async_copy(win.at[0], wg.at[0, y], loc_sem.at[5]),
        pltpu.make_async_copy(win.at[1], wg.at[1, y], loc_sem.at[6]),
    ]
    for copy in local:
        copy.start()

    barrier = pltpu.get_barrier_semaphore()
    for d in (1, 2, 3):
        for dev in (on_x(d), on_y(d), on_z(d)):
            pl.semaphore_signal(barrier, inc=1, device_id=dev, device_id_type=MESH)
    pl.semaphore_signal(barrier, inc=1, device_id=partner, device_id_type=MESH)
    pl.semaphore_wait(barrier, 10)

    def hbm_half(ref, u):
        return lambda part: ref.at[0, pl.ds(part * (T // 2), T // 2), pl.ds(u * CH, CH)]

    q_all, k_all, g_all, d_all, v_all = (
        [gather(on, buf, u, None if src is None else hbm_half(src, u)) for u in range(2)]
        for on, buf, src in (
            (on_x, qg, qin), (on_y, kg, kin), (on_x, gg, gin), (on_x, dv, None), (on_y, vg, None)
        )
    )
    d_sum, v_sum, c_sum = (
        [Sum(on, part, inbox, own, T // 2, (u * CH, CH)) for u in range(2)]
        for on, part, inbox, own in (
            (on_y, d_part, d_in, d_own), (on_x, v_part, v_in, v_own), (on_x, c_part, c_in, c_own)
        )
    )
    i_sum = [Sum(on_z, i_part.at[b], i_in.at[b], i_own.at[b], T // 2, (0, FB)) for b in range(4)]
    w_sum = [Sum(on_y, w_part, w_in, w_mine, FB // 2, (u * CH, CH)) for u in range(2)]
    w_all = Gather(
        on_y, lambda d, part: wg.at[c, wrap(y - d), pl.ds(part * (FB // 2), FB // 2)],
        lambda part: win.at[c, pl.ds(part * (FB // 2), FB // 2)], fixed=True,
    )

    quarter = pl.ds(pl.multiple_of(z * (T // 4), T // 4), T // 4)
    a_x = []

    def spread():
        for d in (1, 3, 2):
            for n in range(4):
                theirs = pl.ds(pl.multiple_of(n * F + wrap(x + d) * FB, FB), FB)
                a_x.append(
                    remote(act.at[0, quarter, theirs], ag.at[d, quarter, pl.ds(n * FB, FB)], on_x(d))
                )

    def z_slot(d, part):
        first = pl.multiple_of(wrap(z - d) * (T // 4) + part * (T // 8), T // 8)
        return ag.at[pl.ds(1, 3), pl.ds(first, T // 8)]

    a_all = Gather(on_z, z_slot, fixed=True, after=a_x)

    ahead = lax.broadcasted_iota(jnp.int32, (T, T), 1) - lax.broadcasted_iota(jnp.int32, (T, T), 0)

    shut = [jnp.where(y >= b, 0.0, NEG) for b in range(4)]

    def scores(u, first, last):
        k_all[u].finish()
        q_all[u].finish()

        def block(a, _):
            p = wrap(x - a)
            cols = pl.ds(pl.multiple_of(a * T, T), T)
            for n in range(2):
                h = 2 * u + n
                hs = slice(h * HD, (h + 1) * HD)
                parts, tops = [], []
                for b in range(4):
                    sc = dot(kg[b, :, hs], qg[a, :, hs], 1, 1)
                    if b == 0:
                        sc = jnp.where(ahead >= (x - p) * T, sc, NEG)
                    parts.append(sc)
                    tops.append(jnp.max(sc, axis=0, keepdims=True) + shut[b])
                top = jnp.maximum(functools.reduce(jnp.maximum, tops), 0.1 * NEG)
                total = jnp.zeros((1, T), F32)
                for b in range(4):
                    pw = jnp.exp2(parts[b] * EXP2_SCALE - (top - shut[b]) * EXP2_SCALE)
                    total = total + jnp.sum(pw, axis=0, keepdims=True)
                    pt[h, b * T:(b + 1) * T, cols] = pw.astype(BF16)
                for m in range(2):
                    st[u, 0, p, 2 * n + m:2 * n + m + 1] = top[:, m * BLOCK:(m + 1) * BLOCK]
                    st[u, 0, p, 4 + 2 * n + m:5 + 2 * n + m] = total[:, m * BLOCK:(m + 1) * BLOCK]
            return 0

        lax.fori_loop(first, last, block, 0)

    st_x = [[], []]

    def send_stats(u):
        for d in (1, 3, 2):
            st_x[u].append(remote(st.at[u, 0], st.at[u, d], on_x(d)))

    def factor(a, h):
        return jnp.concatenate([fa[a, h]] * (HD // 8), axis=0)

    def scale(u):
        need(*st_x[u])
        g_all[u].finish()
        for a in range(4):
            p = wrap(x - a)
            tops = [st[u, d, p, 0:4] for d in range(4)]
            top = functools.reduce(jnp.maximum, tops)
            total = jnp.zeros_like(top)
            for d in range(4):
                total = total + st[u, d, p, 4:8] * jnp.exp2((tops[d] - top) * EXP2_SCALE)
            each = jnp.exp2((tops[0] - top) * EXP2_SCALE) / total
            for n in range(2):
                for m in range(2):
                    row = each[2 * n + m:2 * n + m + 1]
                    fa[a, 2 * u + n, :, m * BLOCK:(m + 1) * BLOCK] = jnp.broadcast_to(row, (8, BLOCK))
        for h in (2 * u, 2 * u + 1):
            hs = slice(h * HD, (h + 1) * HD)
            for a in range(4):
                wide = factor(a, h).T
                gs[a * T:(a + 1) * T, hs] = (gg[a, :, hs].astype(F32) * wide).astype(BF16)

    def d_block(u, e):
        b = (4 - e) % 4
        for h in (2 * u, 2 * u + 1):
            hs = slice(h * HD, (h + 1) * HD)
            part = dot(pt[h, b * T:(b + 1) * T, :], gs[:, hs], 1, 0)
            if e:
                d_part[e - 1, :, hs] = part.astype(BF16)
            else:
                d_own[:, hs] = part

    m_x, w_c = {}, {}

    def image_rows(b, width):
        if b:
            need(m_x[b])
        parts = []
        for n in range(T // BLOCK):
            tile = mg[b, :, n * BLOCK:(n + 1) * BLOCK]
            tile = jnp.concatenate([tile] * (width // BLOCK), axis=1)
            parts += [tile] * (BLOCK // 8)
        return jnp.concatenate(parts, axis=0) == 1

    def i_block(b, e):
        need(*w_c.values())
        for u in range(2):
            if b:
                need(*(d_all[u].near_1, d_all[u].far, d_all[u].near_3)[b - 1])
        n = wrap(z + e)
        rows = dv[b]
        text = dot(rows, wg[0, n], 1, 1)
        image = dot(rows, wg[1, n], 1, 1)
        part = jnp.where(image_rows(b, FB), image, text)
        if e:
            i_part[b, e - 1] = part.astype(BF16)
        else:
            i_own[b] = part

    i_x = {}

    def i_done(b):
        cols = pl.ds(pl.multiple_of(x * FB, FB), FB)
        if b:
            i_sum[b].finish(igs.at[b])
            i_x[b] = remote(igs.at[b], igo.at[:, cols], on_x(-b))
        else:
            i_sum[0].finish(igo.at[:, cols])

    def v_block(e):
        need(*w_c.values())
        a_all.finish()
        b = (4 - e) % 4
        rows = ag[b]
        text = dot(rows, wg[0].reshape(F, C), 1, 0)
        image = dot(rows, wg[1].reshape(F, C), 1, 0)
        part = jnp.where(image_rows(b, C), image, text)
        if e:
            v_part[e - 1] = part.astype(BF16)
        else:
            v_own[...] = part

    def update(kind, u):
        a_all.finish()
        d_all[u].finish()
        cols = slice(u * CH, (u + 1) * CH)
        masked = [
            jnp.where(image_rows(b, CH) == (kind == 1), dv[b, :, cols].astype(F32), 0.0).astype(BF16)
            for b in range(4)
        ]
        return dot(ag[...].reshape(4 * T, F), jnp.concatenate(masked, axis=0), 0, 0)

    def c_block(u, e):
        v_all[u].finish()
        a = (4 - e) % 4
        for h in (2 * u, 2 * u + 1):
            hs = slice(h * HD, (h + 1) * HD)
            values = vg[:, :, hs].reshape(4 * T, HD)
            part = dot(values, pt[h, :, a * T:(a + 1) * T], 0, 0)
            part = (part * factor(a, h)).T
            if e:
                c_part[e - 1, :, hs] = part.astype(BF16)
            else:
                c_own[:, hs] = part

    def d_done(u):
        d_sum[u].finish(dv.at[0])

    def v_done(u):
        v_sum[u].finish(vg.at[0])

    def c_done(u):
        c_sum[u].finish(co)

    def hand(d):
        need(*(w_all.near_1, w_all.far, w_all.near_3)[d - 1])
        block = wg.at[c, wrap(y - d)]
        w_c[d] = remote(block, block, partner)

    w_x, w_back = {}, []

    def w_other_kind(u):
        w_other[u] = update(1 - c, u).astype(BF16)
        w_x[u] = remote(w_other.at[u], w_recv.at[u], partner)

    def w_own_kind(u):
        w_own[u] = update(c, u)

    def w_add(u):
        need(w_x[u])
        cols = slice(u * CH, (u + 1) * CH)
        for e in range(4):
            rows = pl.ds(pl.multiple_of(wrap(y + e) * FB, FB), FB)
            summed = w_own[u, rows, :] + w_recv[u, rows, :].astype(F32)
            if e:
                w_part[e - 1, :, cols] = summed.astype(BF16)
            else:
                w_mine[:, cols] = summed

    def w_done(u):
        w_sum[u].finish(wo.at[c])
        block = wo.at[c, :, pl.ds(u * CH, CH)]
        w_back.append(remote(block, block, partner))

    k_all[0].start()
    spread()
    q_all[0].start()
    k_all[0].ra()
    k_all[0].rb()
    for copy in local:
        copy.wait()
    mg[0] = jnp.broadcast_to(mod_v[...], (8, T))
    for d in (1, 2, 3):
        m_x[d] = remote(mg.at[0], mg.at[d], on_x(d))
    k_all[1].start()
    k_all[1].ra()
    k_all[1].rb()
    w_all.start()
    a_all.start()
    q_all[0].ra()
    q_all[0].rb()
    q_all[1].start()
    scores(0, 0, 2)
    q_all[1].ra()
    q_all[1].rb()
    w_all.ra()
    w_all.rb()
    g_all[0].start()
    scores(0, 2, 4)
    a_all.ra()
    a_all.rb()
    send_stats(0)
    hand(1)
    hand(3)
    scores(1, 0, 2)
    g_all[0].ra()
    g_all[0].rb()
    g_all[1].start()
    scores(1, 2, 4)
    hand(2)
    send_stats(1)
    scale(0)
    d_block(0, 3)
    d_block(0, 2)
    g_all[1].ra()
    g_all[1].rb()
    d_block(0, 0)
    d_sum[0].far()
    d_sum[0].near_dn()
    d_block(0, 1)
    d_sum[0].near_up()
    v_block(2)
    v_sum[0].far()
    v_sum[1].far()
    v_block(1)
    v_sum[0].near_up()
    v_sum[1].near_up()
    v_block(0)
    v_block(3)
    v_sum[0].near_dn()
    v_sum[1].near_dn()
    scale(1)
    d_block(1, 2)
    d_sum[1].far()
    d_sum[0].ra()
    v_sum[0].ra()
    v_sum[0].rb()
    d_sum[0].rb()
    d_block(1, 1)
    d_block(1, 3)
    d_sum[1].near_dn()
    d_block(1, 0)
    d_sum[1].near_up()
    v_sum[1].ra()
    v_sum[1].rb()
    d_sum[1].ra()
    d_sum[1].rb()
    d_done(0)
    d_all[0].start()
    v_done(0)
    v_all[0].start()
    v_done(1)
    v_all[1].start()
    d_done(1)
    d_all[1].start()
    i_block(0, 2)
    i_sum[0].far()
    i_block(0, 0)
    d_all[0].ra()
    d_all[0].rb()
    i_block(0, 1)
    i_sum[0].near_up()
    i_block(0, 3)
    i_sum[0].near_dn()
    v_all[0].ra()
    v_all[0].rb()
    d_all[1].ra()
    d_all[1].rb()
    i_sum[0].ra()
    i_sum[0].rb()
    v_all[1].ra()
    v_all[1].rb()
    i_block(1, 1)
    i_sum[1].near_up()
    i_block(3, 1)
    i_block(3, 3)
    i_sum[3].near_dn()
    i_sum[3].near_up()
    i_block(1, 0)
    i_block(1, 3)
    i_sum[1].near_dn()
    i_block(3, 2)
    w_other_kind(0)
    c_block(0, 1)
    c_block(0, 3)
    c_sum[0].near_dn()
    c_block(0, 2)
    c_sum[0].far()
    i_block(2, 2)
    i_sum[2].far()
    i_block(2, 0)
    w_other_kind(1)
    c_block(1, 0)
    i_sum[3].far()
    c_block(0, 0)
    i_block(1, 2)
    i_sum[1].far()
    c_sum[0].near_up()
    i_block(2, 3)
    i_sum[2].near_dn()
    i_block(3, 0)
    c_block(1, 2)
    c_sum[1].far()
    w_own_kind(0)
    c_sum[0].ra()
    w_add(0)
    w_sum[0].far()
    w_sum[0].near_dn()
    w_sum[0].near_up()
    i_sum[2].rb()
    i_block(2, 1)
    i_sum[2].near_up()
    i_sum[2].ra()
    c_sum[0].rb()
    i_done(0)
    c_block(1, 1)
    i_sum[3].ra()
    i_sum[3].rb()
    c_sum[1].near_up()
    w_own_kind(1)
    w_add(1)
    w_sum[1].far()
    w_sum[1].near_dn()
    w_sum[1].near_up()
    c_block(1, 3)
    i_sum[1].ra()
    i_sum[1].rb()
    c_sum[1].near_dn()
    c_sum[1].rb()
    c_sum[1].ra()
    w_sum[0].ra()
    w_sum[0].rb()
    c_done(0)
    i_done(2)
    w_sum[1].ra()
    w_sum[1].rb()
    i_done(3)
    c_done(1)
    i_done(1)
    w_done(0)
    w_done(1)

    outs = [pltpu.make_async_copy(co, ctx_out, loc_sem.at[0])]
    outs[0].start()
    need(*w_back)
    outs.append(pltpu.make_async_copy(wo, wg_out, loc_sem.at[1]))
    outs[1].start()
    for b in (0, 1, 3, 2):
        if b:
            need(i_x[b])
        cols = pl.ds(pl.multiple_of(wrap(x + b) * FB, FB), FB)
        outs.append(pltpu.make_async_copy(igo.at[:, cols], ig_out.at[:, cols], loc_sem.at[2 + b]))
        outs[-1].start()
    need(*copies)
    for copy in copies:
        copy.wait_send()
    for copy in outs:
        copy.wait()


def shards(activations, modality, query_rows, key_rows, value_weight, context_grad):
    vm = lambda shape, dtype=BF16: pltpu.VMEM(shape, dtype)
    dma = lambda *shape: pltpu.SemaphoreType.DMA(shape)
    any_spec = pl.BlockSpec(memory_space=pl.ANY)
    ring_sum = lambda rows, cols: [vm((3, rows, cols)), vm((6, rows // 2, cols)), vm((rows, cols), F32)]
    ctx, ig, wgrad = pl.pallas_call(
        kernel,
        out_shape=(
            jax.ShapeDtypeStruct((T, C), BF16),
            jax.ShapeDtypeStruct((T, F), BF16),
            jax.ShapeDtypeStruct((2, T, C), F32),
        ),
        in_specs=[any_spec] * 6,
        out_specs=(any_spec,) * 3,
        scratch_shapes=[
            vm((1, T), jnp.int32), vm((4, 8, T), jnp.int32), vm((4, T, F)), vm((2, 4, FB, C)),
            vm((4, T, C)), vm((4, T, C)), vm((4, T, C)), vm((4, T, C)), vm((4, T, C)),
            vm((NH, 4 * T, 4 * T)), vm((2, 4, 4, 8, BLOCK), F32), vm((4, NH, 8, T), F32), vm((4 * T, C)),
            *ring_sum(T, C), *ring_sum(T, C), *ring_sum(T, C), vm((T, C)),
            vm((4, 3, T, FB)), vm((4, 6, T // 2, FB)), vm((4, T, FB), F32), vm((4, T, FB)), vm((T, F)),
            vm((2, F, CH)), vm((2, F, CH)), vm((2, F, CH), F32), vm((FB, C), F32), vm((3, FB, C)), vm((6, FB // 2, C)), vm((2, FB, C), F32),
            dma(11), dma(2, 192),
        ],
        compiler_params=pltpu.CompilerParams(
            collective_id=0, has_side_effects=True, vmem_limit_bytes=60 * 2**20
        ),
        name="routed_attention",
    )(activations, modality, query_rows, key_rows, value_weight, context_grad)
    return tuple(hand_out(ctx[None], ig[None], wgrad))


def hand_out_kernel(*refs):
    sem = refs[-1]
    moves = []
    for src, buf, dst in zip(refs[:3], refs[6:9], refs[3:6]):
        for n in range(src.shape[0]):
            for m in range(2):
                rows = pl.ds(m * 128, 128)
                k = len(moves)
                moves.append((
                    pltpu.make_async_copy(src.at[n, rows], buf.at[n, rows], sem.at[0, k]),
                    pltpu.make_async_copy(buf.at[n, rows], dst.at[n, rows], sem.at[1, k]),
                ))
    for come, _ in moves:
        come.start()
    for come, go in moves:
        come.wait()
        go.start()
    for _, go in moves:
        go.wait()


def hand_out(*arrays):
    any_spec = pl.BlockSpec(memory_space=pl.ANY)
    return pl.pallas_call(
        hand_out_kernel,
        out_shape=tuple(jax.ShapeDtypeStruct(a.shape, a.dtype) for a in arrays),
        in_specs=[any_spec] * 3,
        out_specs=(any_spec,) * 3,
        scratch_shapes=[*(pltpu.VMEM(a.shape, a.dtype) for a in arrays), pltpu.SemaphoreType.DMA((2, 8))],
        name="hand_out",
    )(*arrays)


def solution(mesh):
    return jax.shard_map(
        shards,
        mesh=mesh,
        in_specs=(
            P("dp", "sect", None),
            P("dp", "sect"),
            P("dp", "sect", "head"),
            P("dp", "sect", "head"),
            P(None, "sect", "head"),
            P("dp", "sect", "head"),
        ),
        out_specs=(P("dp", "sect", "head"), P("dp", "sect", "head"), P(None, "sect", "head")),
        check_vma=False,
    )
```

```python
import functools

import jax
import jax.numpy as jnp
from jax import lax
from jax.experimental import pallas as pl
from jax.experimental.pallas import tpu as pltpu
from jax.sharding import PartitionSpec as P

HD = 128
BLOCK = 128
EXP2_SCALE = HD ** (-0.5) * 1.4426950408889634
NEG = -1e30
MESH = pl.DeviceIdType.MESH
F32 = jnp.float32
BF16 = jnp.bfloat16

T = 256
C = 512
F = 1024
FB = 256
NH = C // HD
CH = C // 2


def dot(a, b, ca, cb):
    return lax.dot_general(a, b, (((ca,), (cb,)), ((), ())), preferred_element_type=F32)


def wrap(v):
    return lax.rem(v + 4, 4)


def kernel(
    act, mod, qin, kin, win, gin,
    ctx_out, ig_out, wg_out,
    mod_v, mg, ag, wg, qg, gg, kg, vg, dv,
    pt, st, fa, gs,
    d_part, d_in, d_own,
    v_part, v_in, v_own,
    c_part, c_in, c_own, co,
    i_part, i_in, i_own, igs, igo,
    w_other, w_recv, w_own, w_mine, w_part, w_in, wo,
    loc_sem, sems,
):
    c = lax.axis_index("dp")
    s = lax.axis_index("sect")
    z = lax.axis_index("head")
    y = s // 4
    x = lax.rem(s, 4)

    def on_x(d):
        return (c, y * 4 + wrap(x + d), z)

    def on_y(d):
        return (c, wrap(y + d) * 4 + x, z)

    def on_z(d):
        return (c, s, wrap(z + d))

    partner = (1 - c, s, z)
    copies, arrived = [], set()

    def remote(src, dst, dev):
        n = len(copies)
        copy = pltpu.make_async_remote_copy(
            src_ref=src, dst_ref=dst, send_sem=sems.at[0, n], recv_sem=sems.at[1, n],
            device_id=dev, device_id_type=MESH,
        )
        copies.append(copy)
        copy.start()
        return copy

    def need(*some):
        for copy in some:
            if id(copy) not in arrived:
                arrived.add(id(copy))
                copy.wait_recv()

    class Gather:
        def __init__(self, on, slot, own=None, fixed=False, after=()):
            self.on, self.slot, self.fixed, self.after = on, slot, fixed, after
            self.own = own or (lambda part: slot(0, part))
            self.far = []

        def there(self, d, part, step):
            return self.slot(d, part) if self.fixed else self.slot((d + step) % 4, part)

        def start(self):
            need(*self.after)
            a_up = remote(self.own(0), self.there(0, 0, 1), self.on(1))
            b_dn = remote(self.own(1), self.there(0, 1, -1), self.on(-1))
            b_up = remote(self.own(1), self.there(0, 1, 1), self.on(1))
            a_dn = remote(self.own(0), self.there(0, 0, -1), self.on(-1))
            self.near_1, self.near_3 = (a_up, b_up), (b_dn, a_dn)

        def ra(self):
            need(self.near_1[0])
            self.far.append(remote(self.slot(1, 0), self.there(1, 0, 1), self.on(1)))

        def rb(self):
            need(self.near_3[0])
            self.far.append(remote(self.slot(3, 1), self.there(3, 1, -1), self.on(-1)))

        def finish(self):
            need(*self.near_1, *self.near_3, *self.far)

    def gather(on, buf, u, own=None):
        cols = pl.ds(u * CH, CH)
        return Gather(on, lambda d, part: buf.at[d, pl.ds(part * (T // 2), T // 2), cols], own)

    class Sum:
        def __init__(self, on, part, inbox, own, half, cols):
            self.on, self.own, self.half, self.cols = on, own, half, pl.ds(*cols)
            self.part = lambda e, n: part.at[e - 1, pl.ds(n * half, half), self.cols]
            self.inbox = lambda n: inbox.at[n, :, self.cols]

        def far(self):
            self.f_up = remote(self.part(2, 0), self.inbox(0), self.on(1))
            self.f_dn = remote(self.part(2, 1), self.inbox(1), self.on(-1))

        def near_up(self):
            self.n_up = remote(self.part(1, 1), self.inbox(2), self.on(1))

        def near_dn(self):
            self.n_dn = remote(self.part(3, 0), self.inbox(3), self.on(-1))

        def ra(self):
            need(self.f_up)
            here = self.part(1, 0)
            here[...] = (here[...].astype(F32) + self.inbox(0)[...].astype(F32)).astype(BF16)
            self.s_up = remote(here, self.inbox(4), self.on(1))

        def rb(self):
            need(self.f_dn)
            here = self.part(3, 1)
            here[...] = (here[...].astype(F32) + self.inbox(1)[...].astype(F32)).astype(BF16)
            self.s_dn = remote(here, self.inbox(5), self.on(-1))

        def finish(self, out):
            need(self.n_up, self.n_dn, self.s_up, self.s_dn)
            for n, sources in enumerate(((4, 3), (2, 5))):
                rows = pl.ds(n * self.half, self.half)
                total = self.own[rows, self.cols]
                for source in sources:
                    total = total + self.inbox(source)[...].astype(F32)
                out[rows, self.cols] = total.astype(out.dtype)

    local = [
        pltpu.make_async_copy(mod, mod_v, loc_sem.at[0]),
        *(
            pltpu.make_async_copy(
                act.at[0, :, pl.ds(pl.multiple_of(n * F + x * FB, FB), FB)], ag.at[0, :, pl.ds(n * FB, FB)],
                loc_sem.at[7 + n],
            )
            for n in range(4)
        ),
        pltpu.make_async_copy(qin.at[0], qg.at[0], loc_sem.at[2]),
        pltpu.make_async_copy(kin.at[0], kg.at[0], loc_sem.at[3]),
        pltpu.make_async_copy(gin.at[0], gg.at[0], loc_sem.at[4]),
        pltpu.make_async_copy(win.at[0], wg.at[0, y], loc_sem.at[5]),
        pltpu.make_async_copy(win.at[1], wg.at[1, y], loc_sem.at[6]),
    ]
    for copy in local:
        copy.start()

    barrier = pltpu.get_barrier_semaphore()
    for d in (1, 2, 3):
        for dev in (on_x(d), on_y(d), on_z(d)):
            pl.semaphore_signal(barrier, inc=1, device_id=dev, device_id_type=MESH)
    pl.semaphore_signal(barrier, inc=1, device_id=partner, device_id_type=MESH)
    pl.semaphore_wait(barrier, 10)

    def hbm_half(ref, u):
        return lambda part: ref.at[0, pl.ds(part * (T // 2), T // 2), pl.ds(u * CH, CH)]

    q_all, k_all, g_all, d_all, v_all = (
        [gather(on, buf, u, None if src is None else hbm_half(src, u)) for u in range(2)]
        for on, buf, src in (
            (on_x, qg, qin), (on_y, kg, kin), (on_x, gg, gin), (on_x, dv, None), (on_y, vg, None)
        )
    )
    d_sum, v_sum, c_sum = (
        [Sum(on, part, inbox, own, T // 2, (u * CH, CH)) for u in range(2)]
        for on, part, inbox, own in (
            (on_y, d_part, d_in, d_own), (on_x, v_part, v_in, v_own), (on_x, c_part, c_in, c_own)
        )
    )
    i_sum = [Sum(on_z, i_part.at[b], i_in.at[b], i_own.at[b], T // 2, (0, FB)) for b in range(4)]
    w_sum = [Sum(on_y, w_part, w_in, w_mine, FB // 2, (u * CH, CH)) for u in range(2)]
    w_all = Gather(
        on_y, lambda d, part: wg.at[c, wrap(y - d), pl.ds(part * (FB // 2), FB // 2)],
        lambda part: win.at[c, pl.ds(part * (FB // 2), FB // 2)], fixed=True,
    )

    quarter = pl.ds(pl.multiple_of(z * (T // 4), T // 4), T // 4)
    a_x = []

    def spread():
        for d in (1, 3, 2):
            for n in range(4):
                theirs = pl.ds(pl.multiple_of(n * F + wrap(x + d) * FB, FB), FB)
                a_x.append(
                    remote(act.at[0, quarter, theirs], ag.at[d, quarter, pl.ds(n * FB, FB)], on_x(d))
                )

    def z_slot(d, part):
        first = pl.multiple_of(wrap(z - d) * (T // 4) + part * (T // 8), T // 8)
        return ag.at[pl.ds(1, 3), pl.ds(first, T // 8)]

    a_all = Gather(on_z, z_slot, fixed=True, after=a_x)

    ahead = lax.broadcasted_iota(jnp.int32, (T, T), 1) - lax.broadcasted_iota(jnp.int32, (T, T), 0)

    shut = [jnp.where(y >= b, 0.0, NEG) for b in range(4)]

    def scores(u, first, last):
        k_all[u].finish()
        q_all[u].finish()

        def block(a, _):
            p = wrap(x - a)
            cols = pl.ds(pl.multiple_of(a * T, T), T)
            for n in range(2):
                h = 2 * u + n
                hs = slice(h * HD, (h + 1) * HD)
                parts, tops = [], []
                for b in range(4):
                    sc = dot(kg[b, :, hs], qg[a, :, hs], 1, 1)
                    if b == 0:
                        sc = jnp.where(ahead >= (x - p) * T, sc, NEG)
                    parts.append(sc)
                    tops.append(jnp.max(sc, axis=0, keepdims=True) + shut[b])
                top = jnp.maximum(functools.reduce(jnp.maximum, tops), 0.1 * NEG)
                total = jnp.zeros((1, T), F32)
                for b in range(4):
                    pw = jnp.exp2(parts[b] * EXP2_SCALE - (top - shut[b]) * EXP2_SCALE)
                    total = total + jnp.sum(pw, axis=0, keepdims=True)
                    pt[h, b * T:(b + 1) * T, cols] = pw.astype(BF16)
                for m in range(2):
                    st[u, 0, p, 2 * n + m:2 * n + m + 1] = top[:, m * BLOCK:(m + 1) * BLOCK]
                    st[u, 0, p, 4 + 2 * n + m:5 + 2 * n + m] = total[:, m * BLOCK:(m + 1) * BLOCK]
            return 0

        lax.fori_loop(first, last, block, 0, unroll=True)

    st_x = [[], []]

    def send_stats(u):
        for d in (1, 3, 2):
            st_x[u].append(remote(st.at[u, 0], st.at[u, d], on_x(d)))

    def factor(a, h):
        return jnp.concatenate([fa[a, h]] * (HD // 8), axis=0)

    def scale(u):
        need(*st_x[u])
        g_all[u].finish()
        for a in range(4):
            p = wrap(x - a)
            tops = [st[u, d, p, 0:4] for d in range(4)]
            top = functools.reduce(jnp.maximum, tops)
            total = jnp.zeros_like(top)
            for d in range(4):
                total = total + st[u, d, p, 4:8] * jnp.exp2((tops[d] - top) * EXP2_SCALE)
            each = jnp.exp2((tops[0] - top) * EXP2_SCALE) / total
            for n in range(2):
                for m in range(2):
                    row = each[2 * n + m:2 * n + m + 1]
                    fa[a, 2 * u + n, :, m * BLOCK:(m + 1) * BLOCK] = jnp.broadcast_to(row, (8, BLOCK))
        for h in (2 * u, 2 * u + 1):
            hs = slice(h * HD, (h + 1) * HD)
            for a in range(4):
                wide = factor(a, h).T
                gs[a * T:(a + 1) * T, hs] = (gg[a, :, hs].astype(F32) * wide).astype(BF16)

    def d_block(u, e):
        b = (4 - e) % 4
        for h in (2 * u, 2 * u + 1):
            hs = slice(h * HD, (h + 1) * HD)
            part = dot(pt[h, b * T:(b + 1) * T, :], gs[:, hs], 1, 0)
            if e:
                d_part[e - 1, :, hs] = part.astype(BF16)
            else:
                d_own[:, hs] = part

    m_x, w_c = {}, {}

    def image_rows(b, width):
        if b:
            need(m_x[b])
        parts = []
        for n in range(T // BLOCK):
            tile = mg[b, :, n * BLOCK:(n + 1) * BLOCK]
            tile = jnp.concatenate([tile] * (width // BLOCK), axis=1)
            parts += [tile] * (BLOCK // 8)
        return jnp.concatenate(parts, axis=0) == 1

    def i_block(b, e):
        need(*w_c.values())
        for u in range(2):
            if b:
                need(*(d_all[u].near_1, d_all[u].far, d_all[u].near_3)[b - 1])
        n = wrap(z + e)
        rows = dv[b]
        text = dot(rows, wg[0, n], 1, 1)
        image = dot(rows, wg[1, n], 1, 1)
        part = jnp.where(image_rows(b, FB), image, text)
        if e:
            i_part[b, e - 1] = part.astype(BF16)
        else:
            i_own[b] = part

    i_x = {}

    def i_done(b):
        cols = pl.ds(pl.multiple_of(x * FB, FB), FB)
        if b:
            i_sum[b].finish(igs.at[b])
            i_x[b] = remote(igs.at[b], igo.at[:, cols], on_x(-b))
        else:
            i_sum[0].finish(igo.at[:, cols])

    def v_block(e):
        need(*w_c.values())
        a_all.finish()
        b = (4 - e) % 4
        rows = ag[b]
        text = dot(rows, wg[0].reshape(F, C), 1, 0)
        image = dot(rows, wg[1].reshape(F, C), 1, 0)
        part = jnp.where(image_rows(b, C), image, text)
        if e:
            v_part[e - 1] = part.astype(BF16)
        else:
            v_own[...] = part

    def update(kind, u):
        a_all.finish()
        d_all[u].finish()
        cols = slice(u * CH, (u + 1) * CH)
        masked = [
            jnp.where(image_rows(b, CH) == (kind == 1), dv[b, :, cols].astype(F32), 0.0).astype(BF16)
            for b in range(4)
        ]
        return dot(ag[...].reshape(4 * T, F), jnp.concatenate(masked, axis=0), 0, 0)

    def c_block(u, e):
        v_all[u].finish()
        a = (4 - e) % 4
        for h in (2 * u, 2 * u + 1):
            hs = slice(h * HD, (h + 1) * HD)
            values = vg[:, :, hs].reshape(4 * T, HD)
            part = dot(values, pt[h, :, a * T:(a + 1) * T], 0, 0)
            part = (part * factor(a, h)).T
            if e:
                c_part[e - 1, :, hs] = part.astype(BF16)
            else:
                c_own[:, hs] = part

    def d_done(u):
        d_sum[u].finish(dv.at[0])

    def v_done(u):
        v_sum[u].finish(vg.at[0])

    def c_done(u):
        c_sum[u].finish(co)

    def hand(d):
        need(*(w_all.near_1, w_all.far, w_all.near_3)[d - 1])
        block = wg.at[c, wrap(y - d)]
        w_c[d] = remote(block, block, partner)

    w_x, w_back = {}, []

    def w_other_kind(u):
        w_other[u] = update(1 - c, u).astype(BF16)
        w_x[u] = remote(w_other.at[u], w_recv.at[u], partner)

    def w_own_kind(u):
        w_own[u] = update(c, u)

    def w_add(u):
        need(w_x[u])
        cols = slice(u * CH, (u + 1) * CH)
        for e in range(4):
            rows = pl.ds(pl.multiple_of(wrap(y + e) * FB, FB), FB)
            summed = w_own[u, rows, :] + w_recv[u, rows, :].astype(F32)
            if e:
                w_part[e - 1, :, cols] = summed.astype(BF16)
            else:
                w_mine[:, cols] = summed

    def w_done(u):
        w_sum[u].finish(wo.at[c])
        block = wo.at[c, :, pl.ds(u * CH, CH)]
        w_back.append(remote(block, block, partner))

    k_all[0].start()
    spread()
    q_all[0].start()
    k_all[0].ra()
    k_all[0].rb()
    for copy in local:
        copy.wait()
    mg[0] = jnp.broadcast_to(mod_v[...], (8, T))
    for d in (1, 2, 3):
        m_x[d] = remote(mg.at[0], mg.at[d], on_x(d))
    k_all[1].start()
    k_all[1].ra()
    k_all[1].rb()
    w_all.start()
    a_all.start()
    q_all[0].ra()
    q_all[0].rb()
    q_all[1].start()
    scores(0, 0, 2)
    q_all[1].ra()
    q_all[1].rb()
    w_all.ra()
    w_all.rb()
    g_all[0].start()
    scores(0, 2, 4)
    a_all.ra()
    a_all.rb()
    send_stats(0)
    hand(1)
    hand(3)
    scores(1, 0, 2)
    g_all[0].ra()
    g_all[0].rb()
    g_all[1].start()
    scores(1, 2, 4)
    hand(2)
    send_stats(1)
    scale(0)
    d_block(0, 3)
    d_block(0, 2)
    g_all[1].ra()
    g_all[1].rb()
    d_block(0, 0)
    d_sum[0].far()
    d_sum[0].near_dn()
    d_block(0, 1)
    d_sum[0].near_up()
    v_block(2)
    v_sum[0].far()
    v_sum[1].far()
    v_block(1)
    v_sum[0].near_up()
    v_sum[1].near_up()
    v_block(0)
    v_block(3)
    v_sum[0].near_dn()
    v_sum[1].near_dn()
    scale(1)
    d_block(1, 2)
    d_sum[1].far()
    d_sum[0].ra()
    v_sum[0].ra()
    v_sum[0].rb()
    d_sum[0].rb()
    d_block(1, 1)
    d_block(1, 3)
    d_sum[1].near_dn()
    d_block(1, 0)
    d_sum[1].near_up()
    v_sum[1].ra()
    v_sum[1].rb()
    d_sum[1].ra()
    d_sum[1].rb()
    d_done(0)
    d_all[0].start()
    v_done(0)
    v_all[0].start()
    v_done(1)
    v_all[1].start()
    d_done(1)
    d_all[1].start()
    i_block(0, 2)
    i_sum[0].far()
    i_block(0, 0)
    d_all[0].ra()
    d_all[0].rb()
    i_block(0, 1)
    i_sum[0].near_up()
    i_block(0, 3)
    i_sum[0].near_dn()
    v_all[0].ra()
    v_all[0].rb()
    d_all[1].ra()
    d_all[1].rb()
    i_sum[0].ra()
    i_sum[0].rb()
    v_all[1].ra()
    v_all[1].rb()
    i_block(1, 1)
    i_sum[1].near_up()
    i_block(3, 1)
    i_block(3, 3)
    i_sum[3].near_dn()
    i_sum[3].near_up()
    i_block(1, 0)
    i_block(1, 3)
    i_sum[1].near_dn()
    i_block(3, 2)
    w_other_kind(0)
    c_block(0, 1)
    c_block(0, 3)
    c_sum[0].near_dn()
    c_block(0, 2)
    c_sum[0].far()
    i_block(2, 2)
    i_sum[2].far()
    i_block(2, 0)
    w_other_kind(1)
    c_block(1, 0)
    i_sum[3].far()
    c_block(0, 0)
    i_block(1, 2)
    i_sum[1].far()
    c_sum[0].near_up()
    i_block(2, 3)
    i_sum[2].near_dn()
    i_block(3, 0)
    c_block(1, 2)
    c_sum[1].far()
    w_own_kind(0)
    c_sum[0].ra()
    w_add(0)
    w_sum[0].far()
    w_sum[0].near_dn()
    w_sum[0].near_up()
    i_sum[2].rb()
    i_block(2, 1)
    i_sum[2].near_up()
    i_sum[2].ra()
    c_sum[0].rb()
    i_done(0)
    c_block(1, 1)
    i_sum[3].ra()
    i_sum[3].rb()
    c_sum[1].near_up()
    w_own_kind(1)
    w_add(1)
    w_sum[1].far()
    w_sum[1].near_dn()
    w_sum[1].near_up()
    c_block(1, 3)
    i_sum[1].ra()
    i_sum[1].rb()
    c_sum[1].near_dn()
    c_sum[1].rb()
    c_sum[1].ra()
    w_sum[0].ra()
    w_sum[0].rb()
    c_done(0)
    i_done(2)
    w_sum[1].ra()
    w_sum[1].rb()
    i_done(3)
    c_done(1)
    i_done(1)
    w_done(0)
    w_done(1)

    outs = [pltpu.make_async_copy(co, ctx_out, loc_sem.at[0])]
    outs[0].start()
    need(*w_back)
    outs.append(pltpu.make_async_copy(wo, wg_out, loc_sem.at[1]))
    outs[1].start()
    for b in (0, 1, 3, 2):
        if b:
            need(i_x[b])
        cols = pl.ds(pl.multiple_of(wrap(x + b) * FB, FB), FB)
        outs.append(pltpu.make_async_copy(igo.at[:, cols], ig_out.at[:, cols], loc_sem.at[2 + b]))
        outs[-1].start()
    need(*copies)
    for copy in copies:
        copy.wait_send()
    for copy in outs:
        copy.wait()


def shards(activations, modality, query_rows, key_rows, value_weight, context_grad):
    vm = lambda shape, dtype=BF16: pltpu.VMEM(shape, dtype)
    dma = lambda *shape: pltpu.SemaphoreType.DMA(shape)
    any_spec = pl.BlockSpec(memory_space=pl.ANY)
    ring_sum = lambda rows, cols: [vm((3, rows, cols)), vm((6, rows // 2, cols)), vm((rows, cols), F32)]
    ctx, ig, wgrad = pl.pallas_call(
        kernel,
        out_shape=(
            jax.ShapeDtypeStruct((T, C), BF16),
            jax.ShapeDtypeStruct((T, F), BF16),
            jax.ShapeDtypeStruct((2, T, C), F32),
        ),
        in_specs=[any_spec] * 6,
        out_specs=(any_spec,) * 3,
        scratch_shapes=[
            vm((1, T), jnp.int32), vm((4, 8, T), jnp.int32), vm((4, T, F)), vm((2, 4, FB, C)),
            vm((4, T, C)), vm((4, T, C)), vm((4, T, C)), vm((4, T, C)), vm((4, T, C)),
            vm((NH, 4 * T, 4 * T)), vm((2, 4, 4, 8, BLOCK), F32), vm((4, NH, 8, T), F32), vm((4 * T, C)),
            *ring_sum(T, C), *ring_sum(T, C), *ring_sum(T, C), vm((T, C)),
            vm((4, 3, T, FB)), vm((4, 6, T // 2, FB)), vm((4, T, FB), F32), vm((4, T, FB)), vm((T, F)),
            vm((2, F, CH)), vm((2, F, CH)), vm((2, F, CH), F32), vm((FB, C), F32), vm((3, FB, C)), vm((6, FB // 2, C)), vm((2, FB, C), F32),
            dma(11), dma(2, 192),
        ],
        compiler_params=pltpu.CompilerParams(
            collective_id=0, has_side_effects=True, vmem_limit_bytes=60 * 2**20
        ),
        name="routed_attention",
    )(activations, modality, query_rows, key_rows, value_weight, context_grad)
    return tuple(hand_out(ctx[None], ig[None], wgrad))


def hand_out_kernel(*refs):
    sem = refs[-1]
    moves = []
    for src, buf, dst in zip(refs[:3], refs[6:9], refs[3:6]):
        for n in range(src.shape[0]):
            for m in range(2):
                rows = pl.ds(m * 128, 128)
                k = len(moves)
                moves.append((
                    pltpu.make_async_copy(src.at[n, rows], buf.at[n, rows], sem.at[0, k]),
                    pltpu.make_async_copy(buf.at[n, rows], dst.at[n, rows], sem.at[1, k]),
                ))
    for come, _ in moves:
        come.start()
    for come, go in moves:
        come.wait()
        go.start()
    for _, go in moves:
        go.wait()


def hand_out(*arrays):
    any_spec = pl.BlockSpec(memory_space=pl.ANY)
    return pl.pallas_call(
        hand_out_kernel,
        out_shape=tuple(jax.ShapeDtypeStruct(a.shape, a.dtype) for a in arrays),
        in_specs=[any_spec] * 3,
        out_specs=(any_spec,) * 3,
        scratch_shapes=[*(pltpu.VMEM(a.shape, a.dtype) for a in arrays), pltpu.SemaphoreType.DMA((2, 8))],
        name="hand_out",
    )(*arrays)


def solution(mesh):
    return jax.shard_map(
        shards,
        mesh=mesh,
        in_specs=(
            P("dp", "sect", None),
            P("dp", "sect"),
            P("dp", "sect", "head"),
            P("dp", "sect", "head"),
            P(None, "sect", "head"),
            P("dp", "sect", "head"),
        ),
        out_specs=(P("dp", "sect", "head"), P("dp", "sect", "head"), P(None, "sect", "head")),
        check_vma=False,
    )
```
